128 devices in a mesh: prompt: 4 (over y), resp: 32 (over z, x, core).
Axes of the slice: x: 4, y: 4, z: 4, core: 2. Of those that a mesh axis runs over, the one named last changes fastest.
Arguments:
- prompt_rows: bfloat16 [2048, 5120], P(('prompt', 'resp')), may hold values from -6 to 6
- key_weight: bfloat16 [5120, 512], replicated, may hold values from -0.078125 to 0.078125
- value_weight: bfloat16 [5120, 512], replicated, may hold values from -0.078125 to 0.078125
- queries: bfloat16 [16384, 2560], P(('prompt', 'resp')), may hold values from -180 to 180
- own_keys: bfloat16 [16384, 512], P(('prompt', 'resp')), may hold values from -6 to 6
- own_values: bfloat16 [16384, 512], P(('prompt', 'resp')), may hold values from -6 to 6
- out_grad: bfloat16 [16384, 2560], P(('prompt', 'resp')), may hold values from -24 to 24
- first_length: int32 [128], P(('prompt', 'resp')), may hold values from 16 to 112
- resp_prompt: int32 [128, 2], P(('prompt', 'resp')), may hold values from 0 to 3
Outputs:
- query_grad: bfloat16 [16384, 2560], P(('prompt', 'resp'))
- key_grad: bfloat16 [16384, 512], P(('prompt', 'resp'))
- value_grad: bfloat16 [16384, 512], P(('prompt', 'resp'))
- prompt_grad: bfloat16 [2048, 5120], P(('prompt', 'resp'))
The draws below stay inside these ranges and needn't reach their ends.
All inputs are finite; a program needn't handle non-finite values.
Results may differ from the reference program's by a relative error of at most 0.038.
Values may be sent and summed in bfloat16 or wider, within the bound.
A program may use at most 192 MiB of HBM per device.

```python
import jax
import jax.numpy as jnp
from jax import lax

D = 5120
H = 20
KVH = 4
E = 128
PLEN = 512
ROWS_DEV = 128
PROMPTS = 4
TOKENS = 16384
PROMPT_TOKENS = 2048
N_PROMPT = 4
N_RESP = 32
DEVICES = 128


def own_base(key):
    return jnp.clip(jax.random.normal(jax.random.fold_in(key, 11), (TOKENS, KVH * E), jnp.float32), -6.0, 6.0)


def draw_own_keys(key, part):
    base = own_base(key)
    return base.astype(jnp.bfloat16)


def draw_queries(key, part):
    key = jax.random.fold_in(key, 5)
    noise = 2.5 * jnp.clip(jax.random.normal(key, (TOKENS, H * E), jnp.float32), -6.0, 6.0)
    return noise.astype(jnp.bfloat16)


def plant(drawn, own_key, smallest, largest):
    longest = drawn.shape.index(max(drawn.shape))
    spots = []
    for shift in (0, 1):
        where = [jax.random.randint(jax.random.fold_in(own_key, axis), (), 0, length) for axis, length in enumerate(drawn.shape)]
        where[longest] = (where[longest] + shift) % drawn.shape[longest]
        spots.append(tuple(where))
    return drawn.at[spots[0]].set(smallest).at[spots[1]].set(largest)


def block_levels(key, dims, cuts, low, high):
    loudness = 1.0
    for dim, shards_of in cuts:
        draws = jax.random.uniform(jax.random.fold_in(jax.random.fold_in(key, 6), dim), (shards_of,), jnp.float32, low / len(cuts), high / len(cuts))
        loudness = loudness * jnp.repeat(jnp.exp(draws), dims[dim] // shards_of).reshape((-1,) + (1,) * (len(dims) - 1 - dim))
    return loudness


def scatter_about(rng, extent, scale, reach, cuts=(), kind=jnp.bfloat16):
    array = jax.random.normal(rng, extent, jnp.float32) * scale
    if len(cuts) > 0:
        array = block_levels(rng, extent, cuts, -0.22, 0.18) * array
    return jnp.clip(array, min=-reach, max=reach).astype(kind)


def setup_inputs(seed: int = 0) -> dict:
    streams_of = jax.random.split(jax.random.key(seed), 10)
    return {
        "prompt_rows": scatter_about(streams_of[0], (PROMPT_TOKENS, D), 1.0, 6.0, ((0, 128),)),
        "key_weight": scatter_about(streams_of[1], (D, KVH * E), D ** -0.5, 0.078125),
        "value_weight": scatter_about(streams_of[2], (D, KVH * E), D ** -0.5, 0.078125),
        "queries": draw_queries(jax.random.fold_in(streams_of[9], 71), 0),
        "own_keys": draw_own_keys(jax.random.fold_in(streams_of[9], 71), 0),
        "own_values": scatter_about(streams_of[5], (TOKENS, KVH * E), 1.0, 6.0, ((0, 128),)),
        "out_grad": scatter_about(streams_of[6], (TOKENS, H * E), 4.0, 24.0, ((0, 128),)),
        "first_length": plant(jax.random.randint(streams_of[7], (N_PROMPT * N_RESP,), ROWS_DEV // 8, ROWS_DEV - ROWS_DEV // 8 + 1), jax.random.fold_in(streams_of[7], 1), ROWS_DEV // 8, (ROWS_DEV - ROWS_DEV // 8 + 1) - 1).astype(jnp.int32),
        "resp_prompt": plant(jax.random.randint(streams_of[8], (N_PROMPT * N_RESP, 2), 0, PROMPTS), jax.random.fold_in(streams_of[8], 1), 0, PROMPTS - 1).astype(jnp.int32),
    }


def block_scores(query_heads, key_block):
    keys = key_block.reshape(key_block.shape[0], query_heads.shape[1], E).astype(jnp.float32)
    return jnp.einsum("rkge,jke->kgrj", query_heads.astype(jnp.float32), keys, precision=lax.Precision.HIGHEST) * (E ** -0.5)


def value_products(grad_heads, value_block):
    values = value_block.reshape(value_block.shape[0], grad_heads.shape[1], E).astype(jnp.float32)
    return jnp.einsum("rkge,jke->kgrj", grad_heads.astype(jnp.float32), values, precision=lax.Precision.HIGHEST)


def attend(query_heads, grad_heads, blocks):
    row_max = None
    row_total = None
    for key_block, value_block, visible in blocks:
        scores = jnp.where(visible, block_scores(query_heads, key_block), -jnp.inf)
        block_max = jnp.max(scores, axis=-1)
        if row_max is None:
            row_max = block_max
            row_total = jnp.sum(jnp.exp(scores - row_max[..., None]), axis=-1)
        else:
            new_max = jnp.maximum(row_max, block_max)
            row_total = row_total * jnp.exp(row_max - new_max) + jnp.sum(jnp.exp(scores - new_max[..., None]), axis=-1)
            row_max = new_max

    def probabilities(key_block, visible):
        scores = block_scores(query_heads, key_block)
        return jnp.where(visible, jnp.exp(scores - row_max[..., None]) / row_total[..., None], 0.0)

    delta = jnp.zeros_like(row_max)
    for key_block, value_block, visible in blocks:
        probs_low = probabilities(key_block, visible).astype(jnp.bfloat16)
        delta = delta + jnp.sum(probs_low.astype(jnp.float32) * value_products(grad_heads, value_block), axis=-1)

    query_sum = jnp.zeros(query_heads.shape, jnp.float32)
    block_grads = []
    for key_block, value_block, visible in blocks:
        probs = probabilities(key_block, visible)
        probs_low = probs.astype(jnp.bfloat16).astype(jnp.float32)
        dscores = (probs * (value_products(grad_heads, value_block) - delta[..., None])).astype(jnp.bfloat16).astype(jnp.float32)
        keys = key_block.reshape(key_block.shape[0], query_heads.shape[1], E).astype(jnp.float32)
        query_sum = query_sum + jnp.einsum("kgrj,jke->rkge", dscores, keys, precision=lax.Precision.HIGHEST)
        key_part = jnp.einsum("kgrj,rkge->jke", dscores, query_heads.astype(jnp.float32), precision=lax.Precision.HIGHEST) * (E ** -0.5)
        value_part = jnp.einsum("kgrj,rkge->jke", probs_low, grad_heads.astype(jnp.float32), precision=lax.Precision.HIGHEST)
        block_grads.append((key_part.reshape(key_block.shape[0], -1), value_part.reshape(key_block.shape[0], -1)))
    return query_sum * (E ** -0.5), block_grads


def reference(prompt_rows, key_weight, value_weight, queries, own_keys, own_values, out_grad, first_length, resp_prompt):
    prefix_keys = jnp.dot(prompt_rows, key_weight, preferred_element_type=jnp.float32).astype(jnp.bfloat16)
    prefix_values = jnp.dot(prompt_rows, value_weight, preferred_element_type=jnp.float32).astype(jnp.bfloat16)
    group_size = H // KVH

    def device_step(carry, inputs):
        key_total, value_total = carry
        query_rows, key_rows, value_rows, grad_rows, boundary, prompt_pair = inputs
        row_count = query_rows.shape[0]
        query_heads = query_rows.reshape(row_count, KVH, group_size, E)
        grad_heads = grad_rows.reshape(row_count, KVH, group_size, E)
        position = jnp.arange(row_count, dtype=jnp.int32)
        second = position >= boundary
        own_mask = (second[:, None] == second[None, :]) & (position[None, :] <= position[:, None])
        blocks = [(key_rows, value_rows, own_mask)]
        for slot_index in range(2):
            offset = (prompt_pair[slot_index] * PLEN).astype(jnp.int32)
            seen = jnp.broadcast_to((second == (slot_index == 1))[:, None], (row_count, PLEN))
            blocks.append((lax.dynamic_slice_in_dim(prefix_keys, offset, PLEN, 0), lax.dynamic_slice_in_dim(prefix_values, offset, PLEN, 0), seen))
        query_sum, block_grads = attend(query_heads, grad_heads, blocks)
        for slot_index in range(2):
            offset = (prompt_pair[slot_index] * PLEN).astype(jnp.int32)
            key_total = lax.dynamic_update_slice_in_dim(key_total, lax.dynamic_slice_in_dim(key_total, offset, PLEN, 0) + block_grads[1 + slot_index][0], offset, 0)
            value_total = lax.dynamic_update_slice_in_dim(value_total, lax.dynamic_slice_in_dim(value_total, offset, PLEN, 0) + block_grads[1 + slot_index][1], offset, 0)
        results = (query_sum.reshape(row_count, -1).astype(jnp.bfloat16), block_grads[0][0].astype(jnp.bfloat16), block_grads[0][1].astype(jnp.bfloat16))
        return (key_total, value_total), results

    inputs = (queries.reshape(DEVICES, ROWS_DEV, -1), own_keys.reshape(DEVICES, ROWS_DEV, -1), own_values.reshape(DEVICES, ROWS_DEV, -1), out_grad.reshape(DEVICES, ROWS_DEV, -1), first_length, resp_prompt)
    empty = jnp.zeros((PROMPTS * PLEN, KVH * E), jnp.float32)
    (key_total, value_total), (query_grad, key_grad, value_grad) = lax.scan(device_step, (empty, empty), inputs)
    contract = (((1,), (1,)), ((), ()))
    prompt_grad = lax.dot_general(key_total.astype(jnp.bfloat16), key_weight, contract, preferred_element_type=jnp.float32)
    prompt_grad = prompt_grad + lax.dot_general(value_total.astype(jnp.bfloat16), value_weight, contract, preferred_element_type=jnp.float32)
    return (query_grad.reshape(TOKENS, -1), key_grad.reshape(TOKENS, -1), value_grad.reshape(TOKENS, -1), prompt_grad.astype(jnp.bfloat16))
```

```python
import functools

import jax
import jax.numpy as jnp
from jax import lax
from jax.experimental import pallas as pl
from jax.experimental.pallas import tpu as pltpu
from jax.sharding import PartitionSpec as P

MESH = pl.DeviceIdType.MESH
E = 128
KVH = 4
G = 2
GROUP = 5
ROWS = 128
HALF = 16
SCALE = E ** (-0.5)
LOG2E = 1.4426950408889634
ORDERS = ((0, 1, 2), (1, 2, 0), (2, 0, 1))
ORDER_OF = (((0, 1), (2, 0)), ((1, 2), (0, 2)))


def kernel(
    dims,
    prompt_rows,
    key_weight,
    value_weight,
    queries,
    own_keys,
    own_values,
    out_grad,
    first_length,
    resp_prompt,
    query_grad,
    key_grad,
    value_grad,
    prompt_grad,
    wk,
    wv,
    rows,
    q_in,
    g_in,
    own_in,
    scal_out,
    scal_in,
    scal,
    kv_0,
    kv_1,
    keys_ab,
    values_ab,
    q_ab,
    g_ab,
    scores,
    dprobs,
    probs_t,
    dscores_t,
    parts,
    contrib,
    recv1,
    acc1,
    recv2,
    acc2,
    recv3,
    share,
    final,
    dq_out,
    own_out,
    w_sem,
    in_sem,
    x_send,
    x_recv,
    ag_send,
    ag_recv,
    rs_send,
    rs_recv,
    out_sem,
):
    kv = (kv_0, kv_1)
    ny, nz, nx = dims
    prompts = ny
    plen = nz * nx * 2 * HALF
    depth = key_weight.shape[0]
    kcols = G * E
    qcols = G * GROUP * E
    p_index = lax.axis_index("prompt")
    r_index = lax.axis_index("resp")
    core = lax.rem(r_index, 2)
    chip = lax.div(r_index, 2)
    me = (p_index, lax.div(chip, nx), lax.rem(chip, nx))
    other = 1 - core

    def device(coords, on_core):
        return (coords[0], (coords[1] * nx + coords[2]) * 2 + on_core)

    def shifted(dim, off):
        return lax.rem(me[dim] + off, dims[dim])

    def peer(dim, off):
        coords = list(me)
        coords[dim] = shifted(dim, off)
        return device(coords, core)

    partner = device(me, other)

    steps = 5
    piece = depth // steps
    mine_k = pl.ds(pl.multiple_of(core * kcols, kcols), kcols)
    theirs_k = pl.ds(pl.multiple_of(other * kcols, kcols), kcols)
    mine_q = pl.ds(pl.multiple_of(core * qcols, E), qcols)
    theirs_q = pl.ds(pl.multiple_of(other * qcols, E), qcols)
    my_half = pl.ds(pl.multiple_of(core * HALF, HALF), HALF)

    rows_copy = pltpu.make_async_copy(prompt_rows, rows.at[my_half], in_sem.at[0])
    rows_copy.start()
    w_copies = []
    for s in range(steps):
        at = pl.ds(s * piece, piece)
        pair = (
            pltpu.make_async_copy(key_weight.at[at, mine_k], wk.at[at, mine_k], w_sem.at[0, s]),
            pltpu.make_async_copy(value_weight.at[at, mine_k], wv.at[at, mine_k], w_sem.at[1, s]),
        )
        for c in pair:
            c.start()
        w_copies.append(pair)

    barrier = pltpu.get_barrier_semaphore()
    pl.semaphore_signal(barrier, inc=1, device_id=partner, device_id_type=MESH)
    count = 1
    for dim in range(3):
        for off in range(1, dims[dim]):
            pl.semaphore_signal(barrier, inc=1, device_id=peer(dim, off), device_id_type=MESH)
            count += 1
    pl.semaphore_wait(barrier, count)

    def swap(src, dst, index):
        c = pltpu.make_async_remote_copy(
            src_ref=src, dst_ref=dst, send_sem=x_send.at[index], recv_sem=x_recv.at[index],
            device_id=partner, device_id_type=MESH,
        )
        c.start()
        return c

    rows_swap = swap(prompt_rows, rows.at[my_half], 0)
    lane8 = lax.broadcasted_iota(jnp.int32, (8, 128), 1)
    l_mine = first_length[0]
    a_mine = resp_prompt[0, 0]
    b_mine = resp_prompt[0, 1]
    scal_out[...] = jnp.where(lane8 == 0, l_mine, jnp.where(lane8 == 1, a_mine, b_mine))
    scal_swap = swap(scal_out, scal_in, 1)
    own_swaps = [
        swap(own_keys.at[:, theirs_k], own_in.at[1, 0], 2),
        swap(own_values.at[:, theirs_k], own_in.at[1, 1], 3),
    ]
    q_swap = swap(queries.at[:, theirs_q], q_in.at[1], 4)
    g_swap = swap(out_grad.at[:, theirs_q], g_in.at[1], 5)
    local = [
        pltpu.make_async_copy(own_keys.at[:, mine_k], own_in.at[0, 0], in_sem.at[1]),
        pltpu.make_async_copy(own_values.at[:, mine_k], own_in.at[0, 1], in_sem.at[2]),
        pltpu.make_async_copy(queries.at[:, mine_q], q_in.at[0], in_sem.at[3]),
        pltpu.make_async_copy(out_grad.at[:, mine_q], g_in.at[0], in_sem.at[4]),
    ]
    for c in local:
        c.start()

    rows_copy.wait()
    rows_swap.wait_recv()
    k_proj = jnp.zeros((2 * HALF, kcols), jnp.float32)
    v_proj = jnp.zeros((2 * HALF, kcols), jnp.float32)
    for s in range(steps):
        at = pl.ds(s * piece, piece)
        x = rows[:, at]
        w_copies[s][0].wait()
        k_proj = k_proj + jnp.dot(x, wk[at, mine_k], preferred_element_type=jnp.float32)
        w_copies[s][1].wait()
        v_proj = v_proj + jnp.dot(x, wv[at, mine_k], preferred_element_type=jnp.float32)
    k_proj = k_proj.astype(jnp.bfloat16)
    v_proj = v_proj.astype(jnp.bfloat16)
    for g in range(G):
        for h in range(2):
            at = (slice(h * HALF, (h + 1) * HALF), slice(g * E, (g + 1) * E))
            kv[g][0, h, me[0], me[1], me[2]] = k_proj[at]
            kv[g][1, h, me[0], me[1], me[2]] = v_proj[at]

    pieces = [(g, t, h) for g in range(G) for t in range(2) for h in range(2)]

    def gather_copies(g, t, h, phase):
        order = ORDERS[ORDER_OF[g][t][h]]
        index = [me[0], me[1], me[2]]
        for d in order[:phase]:
            index[d] = slice(None)
        block = kv[g].at[t, h, index[0], index[1], index[2]]
        number = (g * 2 + t) * 2 + h
        return [
            pltpu.make_async_remote_copy(
                src_ref=block, dst_ref=block,
                send_sem=ag_send.at[number, phase, off - 1], recv_sem=ag_recv.at[number, phase, off - 1],
                device_id=peer(order[phase], off), device_id_type=MESH,
            )
            for off in range(1, dims[order[phase]])
        ]

    sends = []
    gathers = {}

    def gather_start(name, phase):
        gathers[name, phase] = gather_copies(*name, phase)
        for c in gathers[name, phase]:
            c.start()
        sends.extend(gathers[name, phase])

    def gather_wait(name, phase):
        for c in gathers[name, phase]:
            c.wait_recv()

    for name in pieces:
        gather_start(name, 0)
    for phase in range(2):
        for name in pieces:
            gather_wait(name, phase)
            gather_start(name, phase + 1)

    late = [
        pltpu.make_async_copy(key_weight.at[:, theirs_k], wk.at[:, theirs_k], w_sem.at[0, steps]),
        pltpu.make_async_copy(value_weight.at[:, theirs_k], wv.at[:, theirs_k], w_sem.at[1, steps]),
    ]
    for c in late:
        c.start()

    scal_swap.wait_recv()
    to_smem = pltpu.make_async_copy(scal_in, scal, in_sem.at[5])
    to_smem.start()
    to_smem.wait()
    first = (l_mine, scal[0, 0])
    prompt_a = (a_mine, scal[0, 1])
    prompt_b = (b_mine, scal[0, 2])
    for c in local:
        c.wait()
    for c in own_swaps:
        c.wait_recv()
    q_swap.wait_recv()
    g_swap.wait_recv()

    sub_j = lax.broadcasted_iota(jnp.int32, (ROWS, E), 0)
    lane_i = lax.broadcasted_iota(jnp.int32, (ROWS, E), 1)
    lane_1 = lax.broadcasted_iota(jnp.int32, (1, E), 1)
    wide = GROUP * E
    total_keys = plen + ROWS

    def attend(g, d):
        boundary = first[d]
        in_a = jnp.where(sub_j < boundary, 1.0, 0.0).astype(jnp.bfloat16)
        in_b = jnp.where(sub_j < boundary, 0.0, 1.0).astype(jnp.bfloat16)
        head_k = slice(g * E, (g + 1) * E)
        for t, dst in ((0, keys_ab), (1, values_ab)):
            for which, prompt in ((0, prompt_a[d]), (1, prompt_b[d])):
                cols = slice(which * E, (which + 1) * E)
                for h in range(2):
                    block = kv[g][t, h, prompt]
                    dst[h * (plen // 2) : (h + 1) * (plen // 2), cols] = block.reshape(plen // 2, E)
                dst[plen:, cols] = own_in[d, t, :, head_k]
        for h in range(GROUP):
            cols = slice((g * GROUP + h) * E, (g * GROUP + h + 1) * E)
            at = slice(h * E, (h + 1) * E)
            q = q_in[d, :, cols]
            q_ab[at, 0:E] = q * in_a
            q_ab[at, E:] = q * in_b
            o = g_in[d, :, cols]
            g_ab[at, 0:E] = o * in_a
            g_ab[at, E:] = o * in_b
        both = (((1,), (1,)), ((), ()))
        scores[...] = lax.dot_general(keys_ab[...], q_ab[...], both, preferred_element_type=jnp.float32)
        dprobs[...] = lax.dot_general(values_ab[...], g_ab[...], both, preferred_element_type=jnp.float32)
        seen = (sub_j <= lane_i) & ((sub_j < boundary) == (lane_i < boundary))
        for h in range(GROUP):
            at = slice(h * E, (h + 1) * E)
            s_pre = scores[:plen, at]
            s_own = jnp.where(seen, scores[plen:, at], -jnp.inf)
            top = jnp.maximum(jnp.max(s_pre, axis=0, keepdims=True), jnp.max(s_own, axis=0, keepdims=True))
            e_pre = jnp.exp2((s_pre - top) * (SCALE * LOG2E))
            e_own = jnp.exp2((s_own - top) * (SCALE * LOG2E))
            total = jnp.sum(e_pre, axis=0, keepdims=True) + jnp.sum(e_own, axis=0, keepdims=True)
            inverse = 1.0 / total
            p_pre = e_pre * inverse
            p_own = e_own * inverse
            low_pre = p_pre.astype(jnp.bfloat16)
            low_own = p_own.astype(jnp.bfloat16)
            probs_t[:plen, at] = low_pre
            probs_t[plen:, at] = low_own
            dp_pre = dprobs[:plen, at]
            dp_own = dprobs[plen:, at]
            delta = jnp.sum(low_pre.astype(jnp.float32) * dp_pre, axis=0, keepdims=True) + jnp.sum(
                low_own.astype(jnp.float32) * dp_own, axis=0, keepdims=True
            )
            dscores_t[:plen, at] = (p_pre * (dp_pre - delta)).astype(jnp.bfloat16)
            dscores_t[plen:, at] = (p_own * (dp_own - delta)).astype(jnp.bfloat16)
        parts[d, 1] = jnp.dot(probs_t[...], g_ab[...], preferred_element_type=jnp.float32)
        parts[d, 0] = jnp.dot(dscores_t[...], q_ab[...], preferred_element_type=jnp.float32)
        dq_t = jnp.dot(keys_ab[...].T, dscores_t[...], preferred_element_type=jnp.float32)
        for h in range(GROUP):
            at = slice(h * E, (h + 1) * E)
            picked = jnp.where(lane_1 < boundary, dq_t[:E, at], dq_t[E:, at]) * SCALE
            cols = slice((g * GROUP + h) * E, (g * GROUP + h + 1) * E)
            dq_out[d, :, cols] = picked.T.astype(jnp.bfloat16)
        own_out[d, 0, :, head_k] = ((parts[d, 0, plen:, :E] + parts[d, 0, plen:, E:]) * SCALE).astype(jnp.bfloat16)
        own_out[d, 1, :, head_k] = (parts[d, 1, plen:, :E] + parts[d, 1, plen:, E:]).astype(jnp.bfloat16)

    def contribute(g):
        for t in range(2):
            unit = SCALE if t == 0 else 1.0
            for h in range(2):
                at = slice(h * (plen // 2), (h + 1) * (plen // 2))
                for p in range(prompts):
                    total = None
                    for d in range(2):
                        for which, prompt in ((0, prompt_a[d]), (1, prompt_b[d])):
                            gate = jnp.where(prompt == p, unit, 0.0).astype(jnp.float32)
                            term = parts[d, t, at, which * E : (which + 1) * E] * gate
                            total = term if total is None else total + term
                    contrib[g, t, h, p] = total.astype(jnp.bfloat16).reshape(nz, nx, HALF, E)

    def scatter_copies(g, t, h, phase):
        order = ORDERS[ORDER_OF[g][t][h]][::-1]
        dim = order[phase]
        number = (g * 2 + t) * 2 + h
        left = [d for d in range(3) if d not in order[:phase]]
        out = []
        for off in range(1, dims[dim]):
            index = tuple(shifted(d, off) if d == dim else slice(None) for d in left)
            if phase == 0:
                src, dst = contrib.at[(g, t, h) + index], recv1.at[g, t, h, off - 1]
            elif phase == 1:
                src, dst = acc1.at[(g, t, h) + index], recv2.at[g, t, h, off - 1]
            else:
                src, dst = acc2.at[(g, t, h) + index], recv3.at[g, t, h, off - 1]
            out.append(
                pltpu.make_async_remote_copy(
                    src_ref=src, dst_ref=dst,
                    send_sem=rs_send.at[number, phase, off - 1], recv_sem=rs_recv.at[number, phase, off - 1],
                    device_id=peer(dim, off), device_id_type=MESH,
                )
            )
        return out

    scatters = {}

    def scatter_start(name, phase):
        scatters[name, phase] = scatter_copies(*name, phase)
        for c in scatters[name, phase]:
            c.start()
        sends.extend(scatters[name, phase])

    def scatter_finish(name, phase):
        order = ORDERS[ORDER_OF[name[0]][name[1]][name[2]]][::-1]
        dim = order[phase]
        left = [d for d in range(3) if d not in order[:phase]]
        for c in scatters[name, phase]:
            c.wait_recv()
        index = tuple(me[d] if d == dim else slice(None) for d in left)
        source, arrived = ((contrib, recv1), (acc1, recv2), (acc2, recv3))[phase]
        total = source[name + index].astype(jnp.float32)
        for off in range(1, dims[dim]):
            total = total + arrived[name + (off - 1,)].astype(jnp.float32)
        if phase < 2:
            (acc1, acc2)[phase][name] = total.astype(jnp.bfloat16)
        else:
            g, t, h = name
            share[h, :, (t * G + g) * E : (t * G + g + 1) * E] = total.astype(jnp.bfloat16)

    def of_head(g):
        return [name for name in pieces if name[0] == g]

    for name in of_head(0):
        gather_wait(name, 2)
    attend(0, 0)
    attend(0, 1)
    contribute(0)
    for name in of_head(0):
        scatter_start(name, 0)
    for name in of_head(1):
        gather_wait(name, 2)
    attend(1, 0)
    for name in of_head(0):
        scatter_finish(name, 0)
        scatter_start(name, 1)
    attend(1, 1)
    contribute(1)
    for name in of_head(1):
        scatter_start(name, 0)
    for name in of_head(0):
        scatter_finish(name, 1)
        scatter_start(name, 2)

    home = [
        pltpu.make_async_copy(dq_out.at[0], query_grad.at[:, mine_q], out_sem.at[0]),
        pltpu.make_async_copy(own_out.at[0, 0], key_grad.at[:, mine_k], out_sem.at[1]),
        pltpu.make_async_copy(own_out.at[0, 1], value_grad.at[:, mine_k], out_sem.at[2]),
    ]
    for c in home:
        c.start()
    away = [
        swap(dq_out.at[1], query_grad.at[:, mine_q], 6),
        swap(own_out.at[1, 0], key_grad.at[:, mine_k], 7),
        swap(own_out.at[1, 1], value_grad.at[:, mine_k], 8),
    ]

    for name in of_head(0):
        scatter_finish(name, 2)
    for phase in range(2):
        for name in of_head(1):
            scatter_finish(name, phase)
            scatter_start(name, phase + 1)
    for name in of_head(1):
        scatter_finish(name, 2)

    final_swap = swap(share.at[other], final.at[core], 9)
    final[core] = share[core]
    for c in late:
        c.wait()
    final_swap.wait_recv()
    x_k = jnp.concatenate([final[0, :, :kcols], final[1, :, :kcols]], axis=1)
    x_v = jnp.concatenate([final[0, :, kcols:], final[1, :, kcols:]], axis=1)
    tile = 512
    both = (((1,), (1,)), ((), ()))
    for n in range(depth // tile):
        at = slice(n * tile, (n + 1) * tile)
        total = lax.dot_general(x_k, wk[at, :], both, preferred_element_type=jnp.float32)
        total = total + lax.dot_general(x_v, wv[at, :], both, preferred_element_type=jnp.float32)
        prompt_grad[:, at] = total.astype(jnp.bfloat16)

    for c in sends:
        c.wait_send()
    for c in [rows_swap, scal_swap, q_swap, g_swap, final_swap] + own_swaps + away:
        c.wait_send()
    for c in home:
        c.wait()
    for c in away:
        c.wait_recv()


def per_device(dims, *arrays):
    ny, nz, nx = dims
    depth = arrays[0].shape[1]
    plen = nz * nx * 2 * HALF
    keys = plen + ROWS
    wide = GROUP * E
    bf16, f32 = jnp.bfloat16, jnp.float32
    most = max(dims) - 1
    assert ny == nz == nx
    n = nx
    vmem = pltpu.VMEM
    hbm = pl.BlockSpec(memory_space=pl.ANY)
    smem = pl.BlockSpec(memory_space=pltpu.SMEM)
    dma = pltpu.SemaphoreType.DMA
    scratch = [
        vmem((depth, KVH * E), bf16),
        vmem((depth, KVH * E), bf16),
        vmem((2 * HALF, depth), bf16),
        vmem((2, ROWS, G * wide), bf16),
        vmem((2, ROWS, G * wide), bf16),
        vmem((2, 2, ROWS, G * E), bf16),
        vmem((8, 128), jnp.int32),
        vmem((8, 128), jnp.int32),
        pltpu.SMEM((8, 128), jnp.int32),
        vmem((2, 2, n, n, n, HALF, E), bf16),
        vmem((2, 2, n, n, n, HALF, E), bf16),
        vmem((keys, 2 * E), bf16),
        vmem((keys, 2 * E), bf16),
        vmem((wide, 2 * E), bf16),
        vmem((wide, 2 * E), bf16),
        vmem((keys, wide), f32),
        vmem((keys, wide), f32),
        vmem((keys, wide), bf16),
        vmem((keys, wide), bf16),
        vmem((2, 2, keys, 2 * E), f32),
        vmem((G, 2, 2, n, n, n, HALF, E), bf16),
        vmem((G, 2, 2, n - 1, n, n, HALF, E), bf16),
        vmem((G, 2, 2, n, n, HALF, E), bf16),
        vmem((G, 2, 2, n - 1, n, HALF, E), bf16),
        vmem((G, 2, 2, n, HALF, E), bf16),
        vmem((G, 2, 2, n - 1, HALF, E), bf16),
        vmem((2, HALF, 2 * G * E), bf16),
        vmem((2, HALF, 2 * G * E), bf16),
        vmem((2, ROWS, G * wide), bf16),
        vmem((2, 2, ROWS, G * E), bf16),
        dma((2, 6)),
        dma((6,)),
        dma((10,)),
        dma((10,)),
        dma((8, 3, most)),
        dma((8, 3, most)),
        dma((8, 3, most)),
        dma((8, 3, most)),
        dma((3,)),
    ]
    shape = jax.ShapeDtypeStruct
    return pl.pallas_call(
        functools.partial(kernel, dims),
        out_shape=(
            shape((ROWS, KVH * wide), bf16),
            shape((ROWS, KVH * E), bf16),
            shape((ROWS, KVH * E), bf16),
            shape((HALF, depth), bf16),
        ),
        in_specs=[hbm] * 7 + [smem] * 2,
        out_specs=(hbm, hbm, hbm, pl.BlockSpec(memory_space=pltpu.VMEM)),
        scratch_shapes=scratch,
        compiler_params=pltpu.CompilerParams(
            collective_id=0, has_side_effects=True, vmem_limit_bytes=56 * 1024 * 1024
        ),
    )(*arrays)


def solution(mesh):
    ny = mesh.shape["prompt"]
    chips = mesh.shape["resp"] // 2
    nx = round(chips**0.5)
    dims = (ny, chips // nx, nx)
    rows = P(("prompt", "resp"), None)
    return jax.shard_map(
        functools.partial(per_device, dims),
        mesh=mesh,
        in_specs=(rows, P(), P(), rows, rows, rows, rows, P(("prompt", "resp")), rows),
        out_specs=(rows, rows, rows, rows),
        check_vma=False,
    )
```

```python
import functools

import jax
import jax.numpy as jnp
from jax import lax
from jax.experimental import pallas as pl
from jax.experimental.pallas import tpu as pltpu
from jax.sharding import PartitionSpec as P

MESH = pl.DeviceIdType.MESH
E = 128
KVH = 4
G = 2
GROUP = 5
ROWS = 128
HALF = 16
SCALE = E ** (-0.5)
LOG2E = 1.4426950408889634
ORDERS = ((0, 1, 2), (1, 2, 0), (2, 0, 1))
ORDER_OF = (((0, 1), (2, 0)), ((1, 2), (0, 2)))


def kernel(
    dims,
    prompt_rows,
    key_weight,
    value_weight,
    queries,
    own_keys,
    own_values,
    out_grad,
    first_length,
    resp_prompt,
    query_grad,
    key_grad,
    value_grad,
    prompt_grad,
    wk,
    wv,
    rows,
    q_in,
    g_in,
    own_in,
    scal_out,
    scal_in,
    scal,
    kv_0,
    kv_1,
    keys_ab,
    values_ab,
    q_ab,
    g_ab,
    scores,
    dprobs,
    probs_t,
    dscores_t,
    parts,
    contrib,
    recv1,
    acc1,
    recv2,
    acc2,
    recv3,
    share,
    final,
    dq_out,
    own_out,
    w_sem,
    in_sem,
    x_send,
    x_recv,
    ag_send,
    ag_recv,
    rs_send,
    rs_recv,
    out_sem,
):
    kv = (kv_0, kv_1)
    ny, nz, nx = dims
    prompts = ny
    plen = nz * nx * 2 * HALF
    depth = key_weight.shape[0]
    kcols = G * E
    qcols = G * GROUP * E
    p_index = lax.axis_index("prompt")
    r_index = lax.axis_index("resp")
    core = lax.rem(r_index, 2)
    chip = lax.div(r_index, 2)
    me = (p_index, lax.div(chip, nx), lax.rem(chip, nx))
    other = 1 - core

    def device(coords, on_core):
        return (coords[0], (coords[1] * nx + coords[2]) * 2 + on_core)

    def shifted(dim, off):
        return lax.rem(me[dim] + off, dims[dim])

    def peer(dim, off):
        coords = list(me)
        coords[dim] = shifted(dim, off)
        return device(coords, core)

    partner = device(me, other)

    steps = 5
    piece = depth // steps
    mine_k = pl.ds(pl.multiple_of(core * kcols, kcols), kcols)
    theirs_k = pl.ds(pl.multiple_of(other * kcols, kcols), kcols)
    mine_q = pl.ds(pl.multiple_of(core * qcols, E), qcols)
    theirs_q = pl.ds(pl.multiple_of(other * qcols, E), qcols)
    my_half = pl.ds(pl.multiple_of(core * HALF, HALF), HALF)

    rows_copy = pltpu.make_async_copy(prompt_rows, rows.at[my_half], in_sem.at[0])
    rows_copy.start()
    w_copies = []
    for s in range(steps):
        at = pl.ds(s * piece, piece)
        pair = (
            pltpu.make_async_copy(key_weight.at[at, mine_k], wk.at[at, mine_k], w_sem.at[0, s]),
            pltpu.make_async_copy(value_weight.at[at, mine_k], wv.at[at, mine_k], w_sem.at[1, s]),
        )
        for c in pair:
            c.start()
        w_copies.append(pair)

    barrier = pltpu.get_barrier_semaphore()
    pl.semaphore_signal(barrier, inc=1, device_id=partner, device_id_type=MESH)
    count = 1
    for dim in range(3):
        for off in range(1, dims[dim]):
            pl.semaphore_signal(barrier, inc=1, device_id=peer(dim, off), device_id_type=MESH)
            count += 1
    pl.semaphore_wait(barrier, count)

    def swap(src, dst, index):
        c = pltpu.make_async_remote_copy(
            src_ref=src, dst_ref=dst, send_sem=x_send.at[index], recv_sem=x_recv.at[index],
            device_id=partner, device_id_type=MESH,
        )
        c.start()
        return c

    rows_swap = swap(prompt_rows, rows.at[my_half], 0)
    lane8 = lax.broadcasted_iota(jnp.int32, (8, 128), 1)
    l_mine = first_length[0]
    a_mine = resp_prompt[0, 0]
    b_mine = resp_prompt[0, 1]
    scal_out[...] = jnp.where(lane8 == 0, l_mine, jnp.where(lane8 == 1, a_mine, b_mine))
    scal_swap = swap(scal_out, scal_in, 1)
    own_swaps = [
        swap(own_keys.at[:, theirs_k], own_in.at[1, 0], 2),
        swap(own_values.at[:, theirs_k], own_in.at[1, 1], 3),
    ]
    q_swap = swap(queries.at[:, theirs_q], q_in.at[1], 4)
    g_swap = swap(out_grad.at[:, theirs_q], g_in.at[1], 5)
    local = [
        pltpu.make_async_copy(own_keys.at[:, mine_k], own_in.at[0, 0], in_sem.at[1]),
        pltpu.make_async_copy(own_values.at[:, mine_k], own_in.at[0, 1], in_sem.at[2]),
        pltpu.make_async_copy(queries.at[:, mine_q], q_in.at[0], in_sem.at[3]),
        pltpu.make_async_copy(out_grad.at[:, mine_q], g_in.at[0], in_sem.at[4]),
    ]
    for c in local:
        c.start()

    rows_copy.wait()
    rows_swap.wait_recv()
    k_proj = jnp.zeros((2 * HALF, kcols), jnp.float32)
    v_proj = jnp.zeros((2 * HALF, kcols), jnp.float32)
    for s in range(steps):
        at = pl.ds(s * piece, piece)
        x = rows[:, at]
        w_copies[s][0].wait()
        k_proj = k_proj + jnp.dot(x, wk[at, mine_k], preferred_element_type=jnp.float32)
        w_copies[s][1].wait()
        v_proj = v_proj + jnp.dot(x, wv[at, mine_k], preferred_element_type=jnp.float32)
    k_proj = k_proj.astype(jnp.bfloat16)
    v_proj = v_proj.astype(jnp.bfloat16)
    for g in range(G):
        for h in range(2):
            at = (slice(h * HALF, (h + 1) * HALF), slice(g * E, (g + 1) * E))
            kv[g][0, h, me[0], me[1], me[2]] = k_proj[at]
            kv[g][1, h, me[0], me[1], me[2]] = v_proj[at]

    pieces = [(g, t, h) for g in range(G) for t in range(2) for h in range(2)]

    def gather_copies(g, t, h, phase):
        order = ORDERS[ORDER_OF[g][t][h]]
        index = [me[0], me[1], me[2]]
        for d in order[:phase]:
            index[d] = slice(None)
        block = kv[g].at[t, h, index[0], index[1], index[2]]
        number = (g * 2 + t) * 2 + h
        return [
            pltpu.make_async_remote_copy(
                src_ref=block, dst_ref=block,
                send_sem=ag_send.at[number, phase, off - 1], recv_sem=ag_recv.at[number, phase, off - 1],
                device_id=peer(order[phase], off), device_id_type=MESH,
            )
            for off in range(1, dims[order[phase]])
        ]

    sends = []
    gathers = {}

    def gather_start(name, phase):
        gathers[name, phase] = gather_copies(*name, phase)
        for c in gathers[name, phase]:
            c.start()
        sends.extend(gathers[name, phase])

    def gather_wait(name, phase):
        for c in gathers[name, phase]:
            c.wait_recv()

    for name in pieces:
        gather_start(name, 0)
    for phase in range(2):
        for name in pieces:
            gather_wait(name, phase)
            gather_start(name, phase + 1)

    late = [
        pltpu.make_async_copy(key_weight.at[:, theirs_k], wk.at[:, theirs_k], w_sem.at[0, steps]),
        pltpu.make_async_copy(value_weight.at[:, theirs_k], wv.at[:, theirs_k], w_sem.at[1, steps]),
    ]
    for c in late:
        c.start()

    scal_swap.wait_recv()
    to_smem = pltpu.make_async_copy(scal_in, scal, in_sem.at[5])
    to_smem.start()
    to_smem.wait()
    first = (l_mine, scal[0, 0])
    prompt_a = (a_mine, scal[0, 1])
    prompt_b = (b_mine, scal[0, 2])
    for c in local:
        c.wait()
    for c in own_swaps:
        c.wait_recv()
    q_swap.wait_recv()
    g_swap.wait_recv()

    sub_j = lax.broadcasted_iota(jnp.int32, (ROWS, E), 0)
    lane_i = lax.broadcasted_iota(jnp.int32, (ROWS, E), 1)
    lane_1 = lax.broadcasted_iota(jnp.int32, (1, E), 1)
    wide = GROUP * E
    total_keys = plen + ROWS

    def attend(g, d):
        boundary = first[d]
        in_a = jnp.where(sub_j < boundary, 1.0, 0.0).astype(jnp.bfloat16)
        in_b = jnp.where(sub_j < boundary, 0.0, 1.0).astype(jnp.bfloat16)
        head_k = slice(g * E, (g + 1) * E)
        for t, dst in ((0, keys_ab), (1, values_ab)):
            for which, prompt in ((0, prompt_a[d]), (1, prompt_b[d])):
                cols = slice(which * E, (which + 1) * E)
                for h in range(2):
                    block = kv[g][t, h, prompt]
                    dst[h * (plen // 2) : (h + 1) * (plen // 2), cols] = block.reshape(plen // 2, E)
                dst[plen:, cols] = own_in[d, t, :, head_k]
        for h in range(GROUP):
            cols = slice((g * GROUP + h) * E, (g * GROUP + h + 1) * E)
            at = slice(h * E, (h + 1) * E)
            q = q_in[d, :, cols]
            q_ab[at, 0:E] = q * in_a
            q_ab[at, E:] = q * in_b
            o = g_in[d, :, cols]
            g_ab[at, 0:E] = o * in_a
            g_ab[at, E:] = o * in_b
        both = (((1,), (1,)), ((), ()))
        scores[...] = lax.dot_general(keys_ab[...], q_ab[...], both, preferred_element_type=jnp.float32)
        dprobs[...] = lax.dot_general(values_ab[...], g_ab[...], both, preferred_element_type=jnp.float32)
        seen = (sub_j <= lane_i) & ((sub_j < boundary) == (lane_i < boundary))
        for h in range(GROUP):
            at = slice(h * E, (h + 1) * E)
            s_pre = scores[:plen, at]
            s_own = jnp.where(seen, scores[plen:, at], -jnp.inf)
            top = jnp.maximum(jnp.max(s_pre, axis=0, keepdims=True), jnp.max(s_own, axis=0, keepdims=True))
            e_pre = jnp.exp2((s_pre - top) * (SCALE * LOG2E))
            e_own = jnp.exp2((s_own - top) * (SCALE * LOG2E))
            total = jnp.sum(e_pre, axis=0, keepdims=True) + jnp.sum(e_own, axis=0, keepdims=True)
            inverse = 1.0 / total
            p_pre = e_pre * inverse
            p_own = e_own * inverse
            low_pre = p_pre.astype(jnp.bfloat16)
            low_own = p_own.astype(jnp.bfloat16)
            probs_t[:plen, at] = low_pre
            probs_t[plen:, at] = low_own
            dp_pre = dprobs[:plen, at]
            dp_own = dprobs[plen:, at]
            delta = jnp.sum(low_pre.astype(jnp.float32) * dp_pre, axis=0, keepdims=True) + jnp.sum(
                low_own.astype(jnp.float32) * dp_own, axis=0, keepdims=True
            )
            dscores_t[:plen, at] = (p_pre * (dp_pre - delta)).astype(jnp.bfloat16)
            dscores_t[plen:, at] = (p_own * (dp_own - delta)).astype(jnp.bfloat16)
        parts[d, 1] = jnp.dot(probs_t[...], g_ab[...], preferred_element_type=jnp.float32)
        parts[d, 0] = jnp.dot(dscores_t[...], q_ab[...], preferred_element_type=jnp.float32)
        dq_t = jnp.dot(keys_ab[...].T, dscores_t[...], preferred_element_type=jnp.float32)
        for h in range(GROUP):
            at = slice(h * E, (h + 1) * E)
            picked = jnp.where(lane_1 < boundary, dq_t[:E, at], dq_t[E:, at]) * SCALE
            cols = slice((g * GROUP + h) * E, (g * GROUP + h + 1) * E)
            dq_out[d, :, cols] = picked.T.astype(jnp.bfloat16)
        own_out[d, 0, :, head_k] = ((parts[d, 0, plen:, :E] + parts[d, 0, plen:, E:]) * SCALE).astype(jnp.bfloat16)
        own_out[d, 1, :, head_k] = (parts[d, 1, plen:, :E] + parts[d, 1, plen:, E:]).astype(jnp.bfloat16)

    def contribute(g):
        for t in range(2):
            unit = SCALE if t == 0 else 1.0
            for h in range(2):
                at = slice(h * (plen // 2), (h + 1) * (plen // 2))
                for p in range(prompts):
                    total = None
                    for d in range(2):
                        for which, prompt in ((0, prompt_a[d]), (1, prompt_b[d])):
                            gate = jnp.where(prompt == p, unit, 0.0).astype(jnp.float32)
                            term = parts[d, t, at, which * E : (which + 1) * E] * gate
                            total = term if total is None else total + term
                    contrib[g, t, h, p] = total.astype(jnp.bfloat16).reshape(nz, nx, HALF, E)

    def scatter_copies(g, t, h, phase):
        order = ORDERS[ORDER_OF[g][t][h]][::-1]
        dim = order[phase]
        number = (g * 2 + t) * 2 + h
        left = [d for d in range(3) if d not in order[:phase]]
        out = []
        for off in range(1, dims[dim]):
            index = tuple(shifted(d, off) if d == dim else slice(None) for d in left)
            if phase == 0:
                src, dst = contrib.at[(g, t, h) + index], recv1.at[g, t, h, off - 1]
            elif phase == 1:
                src, dst = acc1.at[(g, t, h) + index], recv2.at[g, t, h, off - 1]
            else:
                src, dst = acc2.at[(g, t, h) + index], recv3.at[g, t, h, off - 1]
            out.append(
                pltpu.make_async_remote_copy(
                    src_ref=src, dst_ref=dst,
                    send_sem=rs_send.at[number, phase, off - 1], recv_sem=rs_recv.at[number, phase, off - 1],
                    device_id=peer(dim, off), device_id_type=MESH,
                )
            )
        return out

    scatters = {}

    def scatter_start(name, phase):
        scatters[name, phase] = scatter_copies(*name, phase)
        for c in scatters[name, phase]:
            c.start()
        sends.extend(scatters[name, phase])

    def scatter_finish(name, phase):
        order = ORDERS[ORDER_OF[name[0]][name[1]][name[2]]][::-1]
        dim = order[phase]
        left = [d for d in range(3) if d not in order[:phase]]
        for c in scatters[name, phase]:
            c.wait_recv()
        index = tuple(me[d] if d == dim else slice(None) for d in left)
        source, arrived = ((contrib, recv1), (acc1, recv2), (acc2, recv3))[phase]
        total = source[name + index].astype(jnp.float32)
        for off in range(1, dims[dim]):
            total = total + arrived[name + (off - 1,)].astype(jnp.float32)
        if phase < 2:
            (acc1, acc2)[phase][name] = total.astype(jnp.bfloat16)
        else:
            g, t, h = name
            share[h, :, (t * G + g) * E : (t * G + g + 1) * E] = total.astype(jnp.bfloat16)

    def of_head(g):
        return [name for name in pieces if name[0] == g]

    for name in of_head(0):
        gather_wait(name, 2)
    attend(0, 0)
    attend(0, 1)
    contribute(0)
    for name in of_head(0):
        scatter_start(name, 0)
    for name in of_head(1):
        gather_wait(name, 2)
    attend(1, 0)
    attend(1, 1)
    contribute(1)
    for name in of_head(1):
        scatter_start(name, 0)
    for name in of_head(0):
        scatter_finish(name, 0)
        scatter_start(name, 1)

    home = [
        pltpu.make_async_copy(dq_out.at[0], query_grad.at[:, mine_q], out_sem.at[0]),
        pltpu.make_async_copy(own_out.at[0, 0], key_grad.at[:, mine_k], out_sem.at[1]),
        pltpu.make_async_copy(own_out.at[0, 1], value_grad.at[:, mine_k], out_sem.at[2]),
    ]
    for c in home:
        c.start()
    away = [
        swap(dq_out.at[1], query_grad.at[:, mine_q], 6),
        swap(own_out.at[1, 0], key_grad.at[:, mine_k], 7),
        swap(own_out.at[1, 1], value_grad.at[:, mine_k], 8),
    ]

    for name in of_head(1):
        scatter_finish(name, 0)
        scatter_start(name, 1)
    for name in pieces:
        scatter_finish(name, 1)
        scatter_start(name, 2)
    for name in pieces:
        scatter_finish(name, 2)

    final_swap = swap(share.at[other], final.at[core], 9)
    final[core] = share[core]
    for c in late:
        c.wait()
    final_swap.wait_recv()
    x_k = jnp.concatenate([final[0, :, :kcols], final[1, :, :kcols]], axis=1)
    x_v = jnp.concatenate([final[0, :, kcols:], final[1, :, kcols:]], axis=1)
    tile = 512
    both = (((1,), (1,)), ((), ()))
    for n in range(depth // tile):
        at = slice(n * tile, (n + 1) * tile)
        total = lax.dot_general(x_k, wk[at, :], both, preferred_element_type=jnp.float32)
        total = total + lax.dot_general(x_v, wv[at, :], both, preferred_element_type=jnp.float32)
        prompt_grad[:, at] = total.astype(jnp.bfloat16)

    for c in sends:
        c.wait_send()
    for c in [rows_swap, scal_swap, q_swap, g_swap, final_swap] + own_swaps + away:
        c.wait_send()
    for c in home:
        c.wait()
    for c in away:
        c.wait_recv()


def hand_over(*refs):
    sources, results, buffers, arrive, leave = refs[:4], refs[4:8], refs[8:12], refs[12], refs[13]
    inward = [pltpu.make_async_copy(a, b, arrive.at[i]) for i, (a, b) in enumerate(zip(sources, buffers))]
    outward = [pltpu.make_async_copy(b, c, leave.at[i]) for i, (b, c) in enumerate(zip(buffers, results))]
    for c in inward:
        c.start()
    for c, after in zip(inward, outward):
        c.wait()
        after.start()
    for c in outward:
        c.wait()


def per_device(dims, *arrays):
    ny, nz, nx = dims
    depth = arrays[0].shape[1]
    plen = nz * nx * 2 * HALF
    keys = plen + ROWS
    wide = GROUP * E
    bf16, f32 = jnp.bfloat16, jnp.float32
    most = max(dims) - 1
    assert ny == nz == nx
    n = nx
    vmem = pltpu.VMEM
    hbm = pl.BlockSpec(memory_space=pl.ANY)
    smem = pl.BlockSpec(memory_space=pltpu.SMEM)
    dma = pltpu.SemaphoreType.DMA
    scratch = [
        vmem((depth, KVH * E), bf16),
        vmem((depth, KVH * E), bf16),
        vmem((2 * HALF, depth), bf16),
        vmem((2, ROWS, G * wide), bf16),
        vmem((2, ROWS, G * wide), bf16),
        vmem((2, 2, ROWS, G * E), bf16),
        vmem((8, 128), jnp.int32),
        vmem((8, 128), jnp.int32),
        pltpu.SMEM((8, 128), jnp.int32),
        vmem((2, 2, n, n, n, HALF, E), bf16),
        vmem((2, 2, n, n, n, HALF, E), bf16),
        vmem((keys, 2 * E), bf16),
        vmem((keys, 2 * E), bf16),
        vmem((wide, 2 * E), bf16),
        vmem((wide, 2 * E), bf16),
        vmem((keys, wide), f32),
        vmem((keys, wide), f32),
        vmem((keys, wide), bf16),
        vmem((keys, wide), bf16),
        vmem((2, 2, keys, 2 * E), f32),
        vmem((G, 2, 2, n, n, n, HALF, E), bf16),
        vmem((G, 2, 2, n - 1, n, n, HALF, E), bf16),
        vmem((G, 2, 2, n, n, HALF, E), bf16),
        vmem((G, 2, 2, n - 1, n, HALF, E), bf16),
        vmem((G, 2, 2, n, HALF, E), bf16),
        vmem((G, 2, 2, n - 1, HALF, E), bf16),
        vmem((2, HALF, 2 * G * E), bf16),
        vmem((2, HALF, 2 * G * E), bf16),
        vmem((2, ROWS, G * wide), bf16),
        vmem((2, 2, ROWS, G * E), bf16),
        dma((2, 6)),
        dma((6,)),
        dma((10,)),
        dma((10,)),
        dma((8, 3, most)),
        dma((8, 3, most)),
        dma((8, 3, most)),
        dma((8, 3, most)),
        dma((3,)),
    ]
    shape = jax.ShapeDtypeStruct
    results = (
        shape((ROWS, KVH * wide), bf16),
        shape((ROWS, KVH * E), bf16),
        shape((ROWS, KVH * E), bf16),
        shape((HALF, depth), bf16),
    )
    made = pl.pallas_call(
        functools.partial(kernel, dims),
        out_shape=results,
        in_specs=[hbm] * 7 + [smem] * 2,
        out_specs=(hbm, hbm, hbm, pl.BlockSpec(memory_space=pltpu.VMEM)),
        scratch_shapes=scratch,
        compiler_params=pltpu.CompilerParams(
            collective_id=0, has_side_effects=True, vmem_limit_bytes=56 * 1024 * 1024
        ),
    )(*arrays)
    return pl.pallas_call(
        hand_over,
        out_shape=results,
        in_specs=[hbm] * 4,
        out_specs=(hbm,) * 4,
        scratch_shapes=[vmem(r.shape, r.dtype) for r in results] + [dma((4,)), dma((4,))],
    )(*made)


def solution(mesh):
    ny = mesh.shape["prompt"]
    chips = mesh.shape["resp"] // 2
    nx = round(chips**0.5)
    dims = (ny, chips // nx, nx)
    rows = P(("prompt", "resp"), None)
    return jax.shard_map(
        functools.partial(per_device, dims),
        mesh=mesh,
        in_specs=(rows, P(), P(), rows, rows, rows, rows, P(("prompt", "resp")), rows),
        out_specs=(rows, rows, rows, rows),
        check_vma=False,
    )
```

```python
import functools

import jax
import jax.numpy as jnp
from jax import lax
from jax.experimental import pallas as pl
from jax.experimental.pallas import tpu as pltpu
from jax.sharding import PartitionSpec as P

MESH = pl.DeviceIdType.MESH
E = 128
KVH = 4
G = 2
GROUP = 5
ROWS = 128
HALF = 16
SCALE = E ** (-0.5)
LOG2E = 1.4426950408889634
RING = (((0, 1), (2, 0)), ((1, 2), (0, 2)))


def kernel(
    dims,
    prompt_rows,
    key_weight,
    value_weight,
    queries,
    own_keys,
    own_values,
    out_grad,
    first_length,
    resp_prompt,
    query_grad,
    key_grad,
    value_grad,
    prompt_grad,
    wk,
    wv,
    rows,
    q_in,
    g_in,
    own_in,
    scal_out,
    scal_in,
    scal,
    stage,
    kv_00,
    kv_01,
    kv_10,
    kv_11,
    keys_ab,
    values_ab,
    q_ab,
    g_ab,
    probs,
    dprobs,
    probs_t,
    dscores_t,
    parts,
    contrib,
    recv1,
    acc1,
    recv2,
    share,
    final,
    dq_out,
    own_out,
    w_sem,
    in_sem,
    x_send,
    x_recv,
    plane_send,
    plane_recv,
    ring_send,
    ring_recv,
    out_sem,
):
    kv = ((kv_00, kv_01), (kv_10, kv_11))
    n = dims[0]
    prompts = n
    plen = n * n * 2 * HALF
    depth = key_weight.shape[0]
    kcols = G * E
    qcols = G * GROUP * E
    r_index = lax.axis_index("resp")
    core = lax.rem(r_index, 2)
    chip = lax.div(r_index, 2)
    place = (lax.axis_index("prompt"), lax.div(chip, n), lax.rem(chip, n))
    other = 1 - core
    even = core == 0
    turned = (place[1], place[2], place[0])
    me = tuple(jnp.where(even, a, b) for a, b in zip(place, turned))
    partner_me = tuple(jnp.where(even, b, a) for a, b in zip(place, turned))

    def device(coords):
        y = jnp.where(even, coords[0], coords[2])
        z = jnp.where(even, coords[1], coords[0])
        x = jnp.where(even, coords[2], coords[1])
        return (y, (z * n + x) * 2 + core)

    near = [[lax.rem(me[d] + off, n) for off in range(n)] for d in range(3)]

    def peer(*moves):
        coords = list(me)
        for dim, off in moves:
            coords[dim] = near[dim][off]
        return device(coords)

    partner = (place[0], chip * 2 + other)

    steps = 2
    span = depth // steps
    mine_k = pl.ds(pl.multiple_of(core * kcols, kcols), kcols)
    theirs_k = pl.ds(pl.multiple_of(other * kcols, kcols), kcols)
    mine_q = pl.ds(pl.multiple_of(core * qcols, E), qcols)
    theirs_q = pl.ds(pl.multiple_of(other * qcols, E), qcols)

    rows_copy = pltpu.make_async_copy(prompt_rows, rows, in_sem.at[0])
    rows_copy.start()
    w_copies = {}
    for t, (src, dst) in enumerate(((key_weight, wk), (value_weight, wv))):
        for s in range(steps):
            at = pl.ds(s * span, span)
            w_copies[t, s] = pltpu.make_async_copy(src.at[at], dst.at[at], w_sem.at[t, s])
            w_copies[t, s].start()
    local = [
        pltpu.make_async_copy(own_keys.at[:, mine_k], own_in.at[0, 0], in_sem.at[1]),
        pltpu.make_async_copy(own_values.at[:, mine_k], own_in.at[0, 1], in_sem.at[2]),
        pltpu.make_async_copy(queries.at[:, mine_q], q_in.at[0], in_sem.at[3]),
        pltpu.make_async_copy(out_grad.at[:, mine_q], g_in.at[0], in_sem.at[4]),
    ]
    for c in local:
        c.start()

    barrier = pltpu.get_barrier_semaphore()
    pl.semaphore_signal(barrier, inc=1, device_id=partner, device_id_type=MESH)
    greeted = [((d, off),) for d in range(3) for off in range(1, n)]
    greeted += [((d, i), (e, j)) for d in range(3) for e in range(d + 1, 3) for i in range(1, n) for j in range(1, n)]
    for moves in greeted:
        pl.semaphore_signal(barrier, inc=1, device_id=peer(*moves), device_id_type=MESH)

    l_mine = first_length[0]
    a_mine = resp_prompt[0, 0]
    b_mine = resp_prompt[0, 1]
    lane8 = lax.broadcasted_iota(jnp.int32, (8, 128), 1)
    scal_out[...] = jnp.where(lane8 == 0, l_mine, jnp.where(lane8 == 1, a_mine, b_mine))
    rows_copy.wait()
    for t, weight in ((0, wk), (1, wv)):
        total = jnp.zeros((HALF, KVH * E), jnp.float32)
        for s in range(steps):
            w_copies[t, s].wait()
            at = slice(s * span, (s + 1) * span)
            total = total + jnp.dot(rows[:, at], weight[at, :], preferred_element_type=jnp.float32)
        total = total.astype(jnp.bfloat16)
        for head in range(KVH):
            stage[head // G, head % G, t] = total[:, head * E : (head + 1) * E]
    for g in range(G):
        for t in range(2):
            kv[g][t][me[0], me[1], me[2], core] = stage[core, g, t]

    pl.semaphore_wait(barrier, len(greeted) + 1)

    def swap(src, dst, index):
        c = pltpu.make_async_remote_copy(
            src_ref=src, dst_ref=dst, send_sem=x_send.at[index], recv_sem=x_recv.at[index],
            device_id=partner, device_id_type=MESH,
        )
        c.start()
        return c

    kv_swaps = {
        (g, t): swap(
            stage.at[other, g, t], kv[g][t].at[partner_me[0], partner_me[1], partner_me[2], core], g * 2 + t
        )
        for g in range(G)
        for t in range(2)
    }
    scal_swap = swap(scal_out, scal_in, 4)
    q_swap = swap(queries.at[:, theirs_q], q_in.at[1], 5)
    g_swap = swap(out_grad.at[:, theirs_q], g_in.at[1], 6)
    own_swaps = [
        swap(own_keys.at[:, theirs_k], own_in.at[1, 0], 7),
        swap(own_values.at[:, theirs_k], own_in.at[1, 1], 8),
    ]

    def ring_of(name):
        return RING[name[0]][name[1]][name[2]]

    def plane_of(name):
        return [d for d in range(3) if d != ring_of(name)]

    def remote(src, dst, sems, to):
        return pltpu.make_async_remote_copy(
            src_ref=src, dst_ref=dst, send_sem=sems[0], recv_sem=sems[1], device_id=to, device_id_type=MESH
        )

    def plane_sems(phase, g, t):
        return plane_send.at[phase], plane_recv.at[phase, g * 2 + t]

    def ring_sems(phase, g, t):
        return ring_send.at[phase], ring_recv.at[phase, g * 2 + t]

    def plane_arrived(phase, g, t):
        remote(recv2.at[g, t], recv2.at[g, t], plane_sems(phase, g, t), partner).wait_recv()

    def ring_arrived(phase, g, t):
        remote(recv1.at[g, t], recv1.at[g, t], ring_sems(phase, g, t), partner).wait_recv()

    def gather_plane(name):
        g, t, h = name
        a, b = plane_of(name)
        block = kv[g][t].at[me[0], me[1], me[2], h]
        for i in range(n):
            for j in range(n):
                if i + j > 0:
                    remote(block, block, plane_sems(0, g, t), peer((a, i), (b, j))).start()

    def gather_ring(name):
        g, t, h = name
        c = ring_of(name)
        index = [me[d] if d == c else slice(None) for d in range(3)]
        block = kv[g][t].at[index[0], index[1], index[2], h]
        for off in range(1, n):
            remote(block, block, ring_sems(0, g, t), peer((c, off))).start()

    for g in range(G):
        for t in range(2):
            kv_swaps[g, t].wait_recv()
            for h in range(2):
                gather_plane((g, t, h))

    scal_swap.wait_recv()
    to_smem = pltpu.make_async_copy(scal_in, scal, in_sem.at[5])
    to_smem.start()
    to_smem.wait()
    first = (l_mine, scal[0, 0])
    prompt_a = (a_mine, scal[0, 1])
    prompt_b = (b_mine, scal[0, 2])
    for c in local:
        c.wait()
    for c in own_swaps:
        c.wait_recv()
    q_swap.wait_recv()
    g_swap.wait_recv()

    sub_j = lax.broadcasted_iota(jnp.int32, (ROWS, E), 0)
    lane_i = lax.broadcasted_iota(jnp.int32, (ROWS, E), 1)
    lane_1 = lax.broadcasted_iota(jnp.int32, (1, E), 1)
    half_1, half_2 = slice(0, E), slice(E, 2 * E)

    def prepare(g, d):
        in_a = jnp.where(sub_j < first[d], 1.0, 0.0).astype(jnp.bfloat16)
        in_b = jnp.where(sub_j < first[d], 0.0, 1.0).astype(jnp.bfloat16)
        for h in range(GROUP):
            cols = slice((g * GROUP + h) * E, (g * GROUP + h + 1) * E)
            at = slice(h * E, (h + 1) * E)
            for src, dst in ((q_in, q_ab), (g_in, g_ab)):
                value = src[d, :, cols]
                dst[g, d, at, half_1] = value * in_a
                dst[g, d, at, half_2] = value * in_b
        for t, dst in ((0, keys_ab), (1, values_ab)):
            for cols in (half_1, half_2):
                dst[g, d, plen:, cols] = own_in[d, t, :, g * E : (g + 1) * E]

    def fill(g, t, dst):
        def along(axis):
            for d in range(2):
                for cols, prompt in ((half_1, prompt_a[d]), (half_2, prompt_b[d])):
                    block = kv[g][t][prompt] if axis == 0 else kv[g][t][:, :, prompt]
                    dst[g, d, :plen, cols] = block.reshape(plen, E)

        pl.when(even)(lambda: along(0))
        pl.when(core == 1)(lambda: along(2))

    both = (((1,), (1,)), ((), ()))

    def probabilities(g, d):
        boundary = first[d]
        probs[d] = lax.dot_general(keys_ab[g, d], q_ab[g, d], both, preferred_element_type=jnp.float32)
        seen = (sub_j <= lane_i) & ((sub_j < boundary) == (lane_i < boundary))
        for h in range(GROUP):
            at = slice(h * E, (h + 1) * E)
            s_pre = probs[d, :plen, at]
            s_own = jnp.where(seen, probs[d, plen:, at], -jnp.inf)
            top = jnp.maximum(jnp.max(s_pre, axis=0, keepdims=True), jnp.max(s_own, axis=0, keepdims=True))
            e_pre = jnp.exp2((s_pre - top) * (SCALE * LOG2E))
            e_own = jnp.exp2((s_own - top) * (SCALE * LOG2E))
            total = jnp.sum(e_pre, axis=0, keepdims=True) + jnp.sum(e_own, axis=0, keepdims=True)
            inverse = 1.0 / total
            p_pre = e_pre * inverse
            p_own = e_own * inverse
            probs[d, :plen, at] = p_pre
            probs[d, plen:, at] = p_own
            probs_t[d, :plen, at] = p_pre.astype(jnp.bfloat16)
            probs_t[d, plen:, at] = p_own.astype(jnp.bfloat16)
        parts[d] = jnp.dot(probs_t[d], g_ab[g, d], preferred_element_type=jnp.float32)
        own_out[d, 1, :, g * E : (g + 1) * E] = (parts[d, plen:, half_1] + parts[d, plen:, half_2]).astype(jnp.bfloat16)

    def score_gradients(g, d):
        dprobs[...] = lax.dot_general(values_ab[g, d], g_ab[g, d], both, preferred_element_type=jnp.float32)
        for h in range(GROUP):
            at = slice(h * E, (h + 1) * E)
            dp = dprobs[:, at]
            delta = jnp.sum(probs_t[d, :, at].astype(jnp.float32) * dp, axis=0, keepdims=True)
            dscores_t[g, d, :, at] = (probs[d, :, at] * (dp - delta)).astype(jnp.bfloat16)
        parts[d] = jnp.dot(dscores_t[g, d], q_ab[g, d], preferred_element_type=jnp.float32)
        own_out[d, 0, :, g * E : (g + 1) * E] = (
            (parts[d, plen:, half_1] + parts[d, plen:, half_2]) * SCALE
        ).astype(jnp.bfloat16)

    def query_gradients(g, d):
        dq_t = jnp.dot(keys_ab[g, d].T, dscores_t[g, d], preferred_element_type=jnp.float32)
        for h in range(GROUP):
            at = slice(h * E, (h + 1) * E)
            picked = jnp.where(lane_1 < first[d], dq_t[:E, at], dq_t[E:, at]) * SCALE
            cols = slice((g * GROUP + h) * E, (g * GROUP + h + 1) * E)
            dq_out[d, :, cols] = picked.T.astype(jnp.bfloat16)

    def contribute(g, t):
        unit = SCALE if t == 0 else 1.0

        def along(axis):
            for p in range(prompts):
                total = None
                for d in range(2):
                    for cols, prompt in ((half_1, prompt_a[d]), (half_2, prompt_b[d])):
                        gate = jnp.where(prompt == p, unit, 0.0).astype(jnp.float32)
                        term = parts[d, :plen, cols] * gate
                        total = term if total is None else total + term
                block = total.astype(jnp.bfloat16).reshape(n, n, 2, HALF, E)
                if axis == 0:
                    contrib[g, t, p] = block
                else:
                    contrib[g, t, :, :, p] = block

        pl.when(even)(lambda: along(0))
        pl.when(core == 1)(lambda: along(2))

    def scatter_ring(name):
        g, t, h = name
        c = ring_of(name)
        for off in range(1, n):
            index = tuple(near[d][off] if d == c else slice(None) for d in range(3))
            remote(
                contrib.at[(g, t) + index + (h,)], recv1.at[g, t, h, off - 1], ring_sems(1, g, t), peer((c, off))
            ).start()

    def scatter_plane(name):
        g, t, h = name
        c = ring_of(name)
        index = tuple(me[d] if d == c else slice(None) for d in range(3))
        total = contrib[(g, t) + index + (h,)].astype(jnp.float32)
        for off in range(1, n):
            total = total + recv1[g, t, h, off - 1].astype(jnp.float32)
        acc1[g, t, h] = total.astype(jnp.bfloat16)
        a, b = plane_of(name)
        for i in range(n):
            for j in range(n):
                if i + j > 0:
                    remote(
                        acc1.at[g, t, h, near[a][i], near[b][j]], recv2.at[g, t, h, i * n + j - 1],
                        plane_sems(1, g, t), peer((a, i), (b, j)),
                    ).start()

    def scatter_end(name):
        g, t, h = name
        a, b = plane_of(name)
        total = acc1[g, t, h, me[a], me[b]].astype(jnp.float32)
        total = total + jnp.sum(recv2[g, t, h].astype(jnp.float32), axis=0)
        share[h, :, (t * G + g) * E : (t * G + g + 1) * E] = total.astype(jnp.bfloat16)

    for g in range(G):
        for d in range(2):
            prepare(g, d)
    for g in range(G):
        for t in range(2):
            plane_arrived(0, g, t)
            for h in range(2):
                gather_ring((g, t, h))

    for g in range(G):
        ring_arrived(0, g, 0)
        fill(g, 0, keys_ab)
        for d in range(2):
            probabilities(g, d)
        contribute(g, 1)
        for h in range(2):
            scatter_ring((g, 1, h))
        ring_arrived(0, g, 1)
        fill(g, 1, values_ab)
        for d in range(2):
            score_gradients(g, d)
        contribute(g, 0)
        for h in range(2):
            scatter_ring((g, 0, h))

    for g in range(G):
        for d in range(2):
            query_gradients(g, d)
    home = [
        pltpu.make_async_copy(dq_out.at[0], query_grad.at[:, mine_q], out_sem.at[0]),
        pltpu.make_async_copy(own_out.at[0, 0], key_grad.at[:, mine_k], out_sem.at[1]),
        pltpu.make_async_copy(own_out.at[0, 1], value_grad.at[:, mine_k], out_sem.at[2]),
    ]
    for c in home:
        c.start()
    away = [
        swap(dq_out.at[1], query_grad.at[:, mine_q], 9),
        swap(own_out.at[1, 0], key_grad.at[:, mine_k], 10),
        swap(own_out.at[1, 1], value_grad.at[:, mine_k], 11),
    ]

    backwards = [(g, t) for g in range(G) for t in (1, 0)]
    for g, t in backwards:
        ring_arrived(1, g, t)
        for h in range(2):
            scatter_plane((g, t, h))
    for g, t in backwards:
        plane_arrived(1, g, t)
        for h in range(2):
            scatter_end((g, t, h))

    final_swap = swap(share.at[other], final.at[core], 12)
    final[core] = share[core]
    final_swap.wait_recv()
    x_k = jnp.concatenate([final[0, :, :kcols], final[1, :, :kcols]], axis=1)
    x_v = jnp.concatenate([final[0, :, kcols:], final[1, :, kcols:]], axis=1)
    tile = 512
    for s in range(depth // tile):
        at = slice(s * tile, (s + 1) * tile)
        total = lax.dot_general(x_k, wk[at, :], both, preferred_element_type=jnp.float32)
        total = total + lax.dot_general(x_v, wv[at, :], both, preferred_element_type=jnp.float32)
        prompt_grad[:, at] = total.astype(jnp.bfloat16)

    for phase in range(2):
        remote(recv2, recv2, plane_sems(phase, 0, 0), partner).wait_send()
        remote(recv1, recv1, ring_sems(phase, 0, 0), partner).wait_send()
    for c in list(kv_swaps.values()) + own_swaps + away + [scal_swap, q_swap, g_swap, final_swap]:
        c.wait_send()
    for c in home:
        c.wait()
    for c in away:
        c.wait_recv()


def hand_over(*refs):
    sources, results, buffers, arrive, leave = refs[:4], refs[4:8], refs[8:12], refs[12], refs[13]
    inward = [pltpu.make_async_copy(a, b, arrive.at[i]) for i, (a, b) in enumerate(zip(sources, buffers))]
    outward = [pltpu.make_async_copy(b, c, leave.at[i]) for i, (b, c) in enumerate(zip(buffers, results))]
    for c in inward:
        c.start()
    for c, after in zip(inward, outward):
        c.wait()
        after.start()
    for c in outward:
        c.wait()


def per_device(dims, *arrays):
    ny, nz, nx = dims
    depth = arrays[0].shape[1]
    plen = nz * nx * 2 * HALF
    keys = plen + ROWS
    wide = GROUP * E
    bf16, f32 = jnp.bfloat16, jnp.float32
    assert ny == nz == nx
    n = nx
    vmem = pltpu.VMEM
    hbm = pl.BlockSpec(memory_space=pl.ANY)
    smem = pl.BlockSpec(memory_space=pltpu.SMEM)
    dma = pltpu.SemaphoreType.DMA
    scratch = [
        vmem((depth, KVH * E), bf16),
        vmem((depth, KVH * E), bf16),
        vmem((HALF, depth), bf16),
        vmem((2, ROWS, G * wide), bf16),
        vmem((2, ROWS, G * wide), bf16),
        vmem((2, 2, ROWS, G * E), bf16),
        vmem((8, 128), jnp.int32),
        vmem((8, 128), jnp.int32),
        pltpu.SMEM((8, 128), jnp.int32),
        vmem((2, G, 2, HALF, E), bf16),
    ]
    scratch += [vmem((n, n, n, 2, HALF, E), bf16)] * 4
    scratch += [
        vmem((G, 2, keys, 2 * E), bf16),
        vmem((G, 2, keys, 2 * E), bf16),
        vmem((G, 2, wide, 2 * E), bf16),
        vmem((G, 2, wide, 2 * E), bf16),
        vmem((2, keys, wide), f32),
        vmem((keys, wide), f32),
        vmem((2, keys, wide), bf16),
        vmem((G, 2, keys, wide), bf16),
        vmem((2, keys, 2 * E), f32),
        vmem((G, 2, n, n, n, 2, HALF, E), bf16),
        vmem((G, 2, 2, n - 1, n, n, HALF, E), bf16),
        vmem((G, 2, 2, n, n, HALF, E), bf16),
        vmem((G, 2, 2, n * n - 1, HALF, E), bf16),
        vmem((2, HALF, 2 * G * E), bf16),
        vmem((2, HALF, 2 * G * E), bf16),
        vmem((2, ROWS, G * wide), bf16),
        vmem((2, 2, ROWS, G * E), bf16),
        dma((2, 2)),
        dma((6,)),
        dma((13,)),
        dma((13,)),
        dma((2,)),
        dma((2, 2 * G)),
        dma((2,)),
        dma((2, 2 * G)),
        dma((3,)),
    ]
    shape = jax.ShapeDtypeStruct
    results = (
        shape((ROWS, KVH * wide), bf16),
        shape((ROWS, KVH * E), bf16),
        shape((ROWS, KVH * E), bf16),
        shape((HALF, depth), bf16),
    )
    made = pl.pallas_call(
        functools.partial(kernel, dims),
        out_shape=results,
        in_specs=[hbm] * 7 + [smem] * 2,
        out_specs=(hbm, hbm, hbm, pl.BlockSpec(memory_space=pltpu.VMEM)),
        scratch_shapes=scratch,
        compiler_params=pltpu.CompilerParams(
            collective_id=0, has_side_effects=True, vmem_limit_bytes=56 * 1024 * 1024
        ),
    )(*arrays)
    return pl.pallas_call(
        hand_over,
        out_shape=results,
        in_specs=[hbm] * 4,
        out_specs=(hbm,) * 4,
        scratch_shapes=[vmem(r.shape, r.dtype) for r in results] + [dma((4,)), dma((4,))],
    )(*made)


def solution(mesh):
    ny = mesh.shape["prompt"]
    chips = mesh.shape["resp"] // 2
    nx = round(chips**0.5)
    dims = (ny, chips // nx, nx)
    rows = P(("prompt", "resp"), None)
    return jax.shard_map(
        functools.partial(per_device, dims),
        mesh=mesh,
        in_specs=(rows, P(), P(), rows, rows, rows, rows, P(("prompt", "resp")), rows),
        out_specs=(rows, rows, rows, rows),
        check_vma=False,
    )
```

```python
import functools

import jax
import jax.numpy as jnp
from jax import lax
from jax.experimental import pallas as pl
from jax.experimental.pallas import tpu as pltpu
from jax.sharding import PartitionSpec as P

MESH = pl.DeviceIdType.MESH
E = 128
KVH = 4
G = 2
GROUP = 5
ROWS = 128
HALF = 16
SCALE = E ** (-0.5)
LOG2E = 1.4426950408889634
RING = ((0, 1), (2, 0))


def kernel(
    dims,
    prompt_rows,
    key_weight,
    value_weight,
    queries,
    own_keys,
    own_values,
    out_grad,
    first_length,
    resp_prompt,
    query_grad,
    key_grad,
    value_grad,
    prompt_grad,
    wk,
    wv,
    rows,
    q_in,
    g_in,
    own_in,
    scal_out,
    scal_in,
    scal,
    scal_first,
    scal_pair,
    stage,
    planes,
    kv_00,
    kv_01,
    kv_10,
    kv_11,
    keys_ab,
    values_ab,
    q_ab,
    g_ab,
    probs,
    dprobs,
    probs_t,
    dscores_t,
    parts,
    contrib,
    recv1,
    acc1,
    recv2,
    share,
    final,
    w_last,
    prompt_sum,
    prompt_out,
    dq_out,
    own_out,
    w_sem,
    in_sem,
    x_send,
    x_recv,
    hop_send,
    hop_recv,
    plane_send,
    plane_recv,
    ring_send,
    ring_recv,
    out_sem,
):
    kv = ((kv_00, kv_01), (kv_10, kv_11))
    n = dims[0]
    prompts = n
    plen = n * n * 2 * HALF
    depth = key_weight.shape[0]
    kcols = G * E
    qcols = G * GROUP * E
    r_index = lax.axis_index("resp")
    core = lax.rem(r_index, 2)
    chip = lax.div(r_index, 2)
    place = (lax.axis_index("prompt"), lax.div(chip, n), lax.rem(chip, n))
    other = 1 - core
    even = core == 0
    turned = (place[1], place[2], place[0])
    me = tuple(jnp.where(even, a, b) for a, b in zip(place, turned))
    partner_me = tuple(jnp.where(even, b, a) for a, b in zip(place, turned))

    near = [[lax.rem(me[d] + off, n) for off in range(n)] for d in range(3)]
    weight_y = (jnp.where(even, 1, 0), 0, jnp.where(even, 0, 1))
    weight_r = (jnp.where(even, 0, 2 * n), jnp.where(even, 2 * n, 2), jnp.where(even, 2, 0))
    add_y = [[near[d][off] * weight_y[d] for off in range(n)] for d in range(3)]
    add_r = [[near[d][off] * weight_r[d] for off in range(n)] for d in range(3)]

    def peer(*moves):
        off = [0, 0, 0]
        for dim, by in moves:
            off[dim] = by
        y = add_y[0][off[0]] + add_y[2][off[2]]
        r = add_r[0][off[0]] + add_r[1][off[1]] + add_r[2][off[2]] + core
        return (y, r)

    partner = (place[0], chip * 2 + other)

    steps = 2
    span = depth // steps
    mine_k = pl.ds(pl.multiple_of(core * kcols, kcols), kcols)
    theirs_k = pl.ds(pl.multiple_of(other * kcols, kcols), kcols)
    mine_q = pl.ds(pl.multiple_of(core * qcols, E), qcols)
    theirs_q = pl.ds(pl.multiple_of(other * qcols, E), qcols)

    rows_copy = pltpu.make_async_copy(prompt_rows, rows, in_sem.at[0])
    rows_copy.start()
    w_copies = {}
    for t, (src, dst) in enumerate(((key_weight, wk), (value_weight, wv))):
        for s in range(steps):
            at = pl.ds(s * span, span)
            w_copies[t, s] = pltpu.make_async_copy(src.at[at], dst.at[at], w_sem.at[t, s])
            w_copies[t, s].start()
    local = [
        pltpu.make_async_copy(own_keys.at[:, mine_k], own_in.at[0, 0], in_sem.at[1]),
        pltpu.make_async_copy(own_values.at[:, mine_k], own_in.at[0, 1], in_sem.at[2]),
        pltpu.make_async_copy(queries.at[:, mine_q], q_in.at[0], in_sem.at[3]),
        pltpu.make_async_copy(out_grad.at[:, mine_q], g_in.at[0], in_sem.at[4]),
    ]

    barrier = pltpu.get_barrier_semaphore()
    pl.semaphore_signal(barrier, inc=1, device_id=partner, device_id_type=MESH)
    greeted = [((d, off),) for d in range(3) for off in range(1, n)]
    greeted += [((d, i), (e, j)) for d in range(3) for e in range(d + 1, 3) for i in range(1, n) for j in range(1, n)]
    for moves in greeted:
        pl.semaphore_signal(barrier, inc=1, device_id=peer(*moves), device_id_type=MESH)
    scal_copies = [
        pltpu.make_async_copy(first_length, scal_first, in_sem.at[6]),
        pltpu.make_async_copy(resp_prompt, scal_pair, in_sem.at[7]),
    ]
    for c in scal_copies + local:
        c.start()

    for c in scal_copies:
        c.wait()
    l_mine = scal_first[0]
    a_mine = scal_pair[0, 0]
    b_mine = scal_pair[0, 1]
    lane8 = lax.broadcasted_iota(jnp.int32, (8, 128), 1)
    scal_out[...] = jnp.where(lane8 == 0, l_mine, jnp.where(lane8 == 1, a_mine, b_mine))
    rows_copy.wait()
    for t, weight in ((0, wk), (1, wv)):
        total = jnp.zeros((HALF, KVH * E), jnp.float32)
        for s in range(steps):
            w_copies[t, s].wait()
            at = slice(s * span, (s + 1) * span)
            total = total + jnp.dot(rows[:, at], weight[at, :], preferred_element_type=jnp.float32)
        total = total.astype(jnp.bfloat16)
        for head in range(KVH):
            stage[head // G, head % G, t] = total[:, head * E : (head + 1) * E]

    def plane_of(piece):
        return [d for d in range(3) if d != RING[piece[0]][piece[1]]]

    def plane_place(g, at):
        zero, one = plane_of((g, 0)), plane_of((g, 1))
        return tuple(jnp.where(even, at[i], at[j]) for i, j in zip(zero, one))

    for g in range(G):
        a, b = plane_place(g, me)
        planes[g, core, a, b] = stage[core, g]

    pl.semaphore_wait(barrier, len(greeted) + 1)

    def swap(src, dst, index):
        c = pltpu.make_async_remote_copy(
            src_ref=src, dst_ref=dst, send_sem=x_send.at[index], recv_sem=x_recv.at[index],
            device_id=partner, device_id_type=MESH,
        )
        c.start()
        return c

    kv_swaps = []
    for g in range(G):
        a, b = plane_place(g, partner_me)
        kv_swaps.append(swap(stage.at[other, g], planes.at[g, core, a, b], g))

    def remote(src, dst, sems, to):
        return pltpu.make_async_remote_copy(
            src_ref=src, dst_ref=dst, send_sem=sems[0], recv_sem=sems[1], device_id=to, device_id_type=MESH
        )

    def hop_sems(g):
        return hop_send.at[0], hop_recv.at[g]

    def plane_sems(g, t):
        return plane_send.at[0], plane_recv.at[g * 2 + t]

    def ring_sems(phase, g, t):
        return ring_send.at[phase], ring_recv.at[phase, g * 2 + t]

    def hop_arrived(g):
        remote(recv2.at[g], recv2.at[g], hop_sems(g), partner).wait_recv()

    def plane_arrived(g, t):
        remote(recv2.at[g, t], recv2.at[g, t], plane_sems(g, t), partner).wait_recv()

    def ring_arrived(phase, g, t):
        remote(recv1.at[g, t], recv1.at[g, t], ring_sems(phase, g, t), partner).wait_recv()

    beyond = [(i, j) for i in range(n) for j in range(n) if i + j > 0]

    def gather_plane(g):
        for h in range(2):
            a, b = plane_of((g, h))
            block = planes.at[g, h, me[a], me[b]]
            for i, j in beyond:
                remote(block, block, hop_sems(g), peer((a, i), (b, j))).start()

    def gather_ring(g, t, h):
        c = RING[g][h]
        index = tuple(me[d] if d == c else slice(None) for d in range(3)) + (h,)
        for off in range(1, n):
            remote(planes.at[g, h, :, :, t], kv[g][t].at[index], ring_sems(0, g, t), peer((c, off))).start()
        kv[g][t][index] = planes[g, h, :, :, t]

    for g in range(G):
        kv_swaps[g].wait_recv()
        gather_plane(g)
    scal_swap = swap(scal_out, scal_in, 4)
    q_swap = swap(queries.at[:, theirs_q], q_in.at[1], 5)
    g_swap = swap(out_grad.at[:, theirs_q], g_in.at[1], 6)
    own_swaps = [
        swap(own_keys.at[:, theirs_k], own_in.at[1, 0], 7),
        swap(own_values.at[:, theirs_k], own_in.at[1, 1], 8),
    ]
    scal_swap.wait_recv()
    to_smem = pltpu.make_async_copy(scal_in, scal, in_sem.at[5])
    to_smem.start()
    to_smem.wait()
    first = (l_mine, scal[0, 0])
    prompt_a = (a_mine, scal[0, 1])
    prompt_b = (b_mine, scal[0, 2])
    for c in local:
        c.wait()
    for c in own_swaps:
        c.wait_recv()
    q_swap.wait_recv()
    g_swap.wait_recv()

    sub_j = lax.broadcasted_iota(jnp.int32, (ROWS, E), 0)
    lane_i = lax.broadcasted_iota(jnp.int32, (ROWS, E), 1)
    lane_1 = lax.broadcasted_iota(jnp.int32, (1, E), 1)
    half_1, half_2 = slice(0, E), slice(E, 2 * E)

    def prepare(g, d):
        in_a = jnp.where(sub_j < first[d], 1.0, 0.0).astype(jnp.bfloat16)
        in_b = jnp.where(sub_j < first[d], 0.0, 1.0).astype(jnp.bfloat16)
        for h in range(GROUP):
            cols = slice((g * GROUP + h) * E, (g * GROUP + h + 1) * E)
            at = slice(h * E, (h + 1) * E)
            for src, dst in ((q_in, q_ab), (g_in, g_ab)):
                value = src[d, :, cols]
                dst[g, d, at, half_1] = value * in_a
                dst[g, d, at, half_2] = value * in_b
        for t, dst in ((0, keys_ab), (1, values_ab)):
            for cols in (half_1, half_2):
                dst[g, d, plen:, cols] = own_in[d, t, :, g * E : (g + 1) * E]

    def fill(g, t, dst):
        def along(axis):
            for d in range(2):
                for cols, prompt in ((half_1, prompt_a[d]), (half_2, prompt_b[d])):
                    block = kv[g][t][prompt] if axis == 0 else kv[g][t][:, :, prompt]
                    dst[g, d, :plen, cols] = block.reshape(plen, E)

        pl.when(even)(lambda: along(0))
        pl.when(core == 1)(lambda: along(2))

    both = (((1,), (1,)), ((), ()))

    def scores(g, d):
        probs[d] = lax.dot_general(keys_ab[g, d], q_ab[g, d], both, preferred_element_type=jnp.float32)

    def probabilities(g, d):
        boundary = first[d]
        seen = (sub_j <= lane_i) & ((sub_j < boundary) == (lane_i < boundary))
        for h in range(GROUP):
            at = slice(h * E, (h + 1) * E)
            s_pre = probs[d, :plen, at]
            s_own = jnp.where(seen, probs[d, plen:, at], -jnp.inf)
            top = jnp.maximum(jnp.max(s_pre, axis=0, keepdims=True), jnp.max(s_own, axis=0, keepdims=True))
            e_pre = jnp.exp2((s_pre - top) * (SCALE * LOG2E))
            e_own = jnp.exp2((s_own - top) * (SCALE * LOG2E))
            total = jnp.sum(e_pre, axis=0, keepdims=True) + jnp.sum(e_own, axis=0, keepdims=True)
            inverse = 1.0 / total
            p_pre = e_pre * inverse
            p_own = e_own * inverse
            probs[d, :plen, at] = p_pre
            probs[d, plen:, at] = p_own
            probs_t[d, :plen, at] = p_pre.astype(jnp.bfloat16)
            probs_t[d, plen:, at] = p_own.astype(jnp.bfloat16)
        parts[d] = jnp.dot(probs_t[d], g_ab[g, d], preferred_element_type=jnp.float32)
        own_out[d, 1, :, g * E : (g + 1) * E] = (parts[d, plen:, half_1] + parts[d, plen:, half_2]).astype(jnp.bfloat16)

    def prob_gradients(g, d):
        dprobs[d] = lax.dot_general(values_ab[g, d], g_ab[g, d], both, preferred_element_type=jnp.float32)

    def score_gradients(g, d):
        for h in range(GROUP):
            at = slice(h * E, (h + 1) * E)
            dp = dprobs[d, :, at]
            delta = jnp.sum(probs_t[d, :, at].astype(jnp.float32) * dp, axis=0, keepdims=True)
            dscores_t[g, d, :, at] = (probs[d, :, at] * (dp - delta)).astype(jnp.bfloat16)
        parts[d] = jnp.dot(dscores_t[g, d], q_ab[g, d], preferred_element_type=jnp.float32)
        own_out[d, 0, :, g * E : (g + 1) * E] = (
            (parts[d, plen:, half_1] + parts[d, plen:, half_2]) * SCALE
        ).astype(jnp.bfloat16)

    def query_gradients(g, d):
        dq_t = jnp.dot(keys_ab[g, d].T, dscores_t[g, d], preferred_element_type=jnp.float32)
        for h in range(GROUP):
            at = slice(h * E, (h + 1) * E)
            picked = jnp.where(lane_1 < first[d], dq_t[:E, at], dq_t[E:, at]) * SCALE
            cols = slice((g * GROUP + h) * E, (g * GROUP + h + 1) * E)
            dq_out[d, :, cols] = picked.T.astype(jnp.bfloat16)

    def contribute(g, t):
        unit = SCALE if t == 0 else 1.0

        def along(axis):
            for p in range(prompts):
                total = None
                for d in range(2):
                    for cols, prompt in ((half_1, prompt_a[d]), (half_2, prompt_b[d])):
                        gate = jnp.where(prompt == p, unit, 0.0).astype(jnp.float32)
                        term = parts[d, :plen, cols] * gate
                        total = term if total is None else total + term
                block = total.astype(jnp.bfloat16).reshape(n, n, 2, HALF, E)
                if axis == 0:
                    contrib[g, t, p] = block
                else:
                    contrib[g, t, :, :, p] = block

        pl.when(even)(lambda: along(0))
        pl.when(core == 1)(lambda: along(2))

    def scatter_ring(g, t, h):
        c = RING[g][h]
        for off in range(1, n):
            index = tuple(near[d][off] if d == c else slice(None) for d in range(3))
            remote(
                contrib.at[(g, t) + index + (h,)], recv1.at[g, t, h, off - 1], ring_sems(1, g, t), peer((c, off))
            ).start()

    def scatter_plane(g, t):
        ring_arrived(1, g, t)
        for h in range(2):
            c = RING[g][h]
            index = tuple(me[d] if d == c else slice(None) for d in range(3))
            total = contrib[(g, t) + index + (h,)].astype(jnp.float32)
            for off in range(1, n):
                total = total + recv1[g, t, h, off - 1].astype(jnp.float32)
            acc1[g, t, h] = total.astype(jnp.bfloat16)
            a, b = plane_of((g, h))
            for i, j in beyond:
                remote(
                    acc1.at[g, t, h, near[a][i], near[b][j]], recv2.at[g, t, h, i * n + j - 1], plane_sems(g, t),
                    peer((a, i), (b, j)),
                ).start()

    def scatter_end(g, t):
        plane_arrived(g, t)
        for h in range(2):
            a, b = plane_of((g, h))
            total = acc1[g, t, h, me[a], me[b]].astype(jnp.float32)
            total = total + jnp.sum(recv2[g, t, h].astype(jnp.float32), axis=0)
            share[g, t, h] = total.astype(jnp.bfloat16)
        c = swap(share.at[g, t, other], final.at[g, t, core], 12 + g * 2 + t)
        final[g, t, core] = share[g, t, core]
        return c

    for g in range(G):
        for d in range(2):
            prepare(g, d)
    for g in range(G):
        hop_arrived(g)
        for t in range(2):
            for h in range(2):
                gather_ring(g, t, h)

    for g in range(G):
        ring_arrived(0, g, 0)
        fill(g, 0, keys_ab)
        for d in range(2):
            scores(g, d)
        for d in range(2):
            probabilities(g, d)
        contribute(g, 1)
        for h in range(2):
            scatter_ring(g, 1, h)
        ring_arrived(0, g, 1)
        fill(g, 1, values_ab)
        for d in range(2):
            prob_gradients(g, d)
        for d in range(2):
            score_gradients(g, d)
        contribute(g, 0)
        for h in range(2):
            scatter_ring(g, 0, h)

    for d in range(2):
        query_gradients(0, d)
    for t in (1, 0):
        scatter_plane(0, t)
    for d in range(2):
        query_gradients(1, d)
    for t in (1, 0):
        scatter_plane(1, t)
    home = [
        pltpu.make_async_copy(dq_out.at[0], query_grad.at[:, mine_q], out_sem.at[0]),
        pltpu.make_async_copy(own_out.at[0, 0], key_grad.at[:, mine_k], out_sem.at[1]),
        pltpu.make_async_copy(own_out.at[0, 1], value_grad.at[:, mine_k], out_sem.at[2]),
    ]
    for c in home:
        c.start()
    away = [
        swap(dq_out.at[1], query_grad.at[:, mine_q], 9),
        swap(own_out.at[1, 0], key_grad.at[:, mine_k], 10),
        swap(own_out.at[1, 1], value_grad.at[:, mine_k], 11),
    ]

    tile = 512
    tiles = [slice(i * tile, (i + 1) * tile) for i in range(depth // tile)]

    def last_product(g, t, at):
        weight = (wk, wv)[t]
        total = None
        for c in range(2):
            head = slice((c * G + g) * E, (c * G + g + 1) * E)
            term = lax.dot_general(final[g, t, c], weight[at, head], both, preferred_element_type=jnp.float32)
            total = term if total is None else total + term
        return total

    for c in range(2):
        w_last[:, c * E : (c + 1) * E] = wk[:, (c * G + 1) * E : (c * G + 2) * E]

    final_swaps = [scatter_end(0, 1), scatter_end(0, 0)]
    for c in final_swaps:
        c.wait_recv()
    for at in tiles:
        prompt_sum[:, at] = last_product(0, 1, at) + last_product(0, 0, at)
    final_swaps.append(scatter_end(1, 1))
    final_swaps[2].wait_recv()
    for at in tiles:
        prompt_sum[:, at] = prompt_sum[:, at] + last_product(1, 1, at)
    final_swaps.append(scatter_end(1, 0))
    final_swaps[3].wait_recv()
    x_last = jnp.concatenate([final[1, 0, 0], final[1, 0, 1]], axis=1)
    prompt_copies = []
    parted = len(tiles) // 2
    for k, group in enumerate((tiles[:parted], tiles[parted:])):
        for at in group:
            total = lax.dot_general(x_last, w_last[at, :], both, preferred_element_type=jnp.float32)
            prompt_out[:, at] = (prompt_sum[:, at] + total).astype(jnp.bfloat16)
        whole = slice(group[0].start, group[-1].stop)
        prompt_copies.append(
            pltpu.make_async_copy(prompt_out.at[:, whole], prompt_grad.at[:, whole], out_sem.at[3 + k])
        )
        prompt_copies[k].start()

    for phase in range(2):
        remote(recv1, recv1, ring_sems(phase, 0, 0), partner).wait_send()
    remote(recv2, recv2, hop_sems(0), partner).wait_send()
    remote(recv2, recv2, plane_sems(0, 0), partner).wait_send()
    for c in kv_swaps + own_swaps + away + [scal_swap, q_swap, g_swap] + final_swaps:
        c.wait_send()
    for c in home + prompt_copies:
        c.wait()
    for c in away:
        c.wait_recv()


def hand_over(*refs):
    sources, results, buffers, arrive, leave = refs[:4], refs[4:8], refs[8:12], refs[12], refs[13]
    inward = [pltpu.make_async_copy(a, b, arrive.at[i]) for i, (a, b) in enumerate(zip(sources, buffers))]
    outward = [pltpu.make_async_copy(b, c, leave.at[i]) for i, (b, c) in enumerate(zip(buffers, results))]
    for c in inward:
        c.start()
    for c, after in zip(inward, outward):
        c.wait()
        after.start()
    for c in outward:
        c.wait()


def per_device(dims, *arrays):
    ny, nz, nx = dims
    depth = arrays[0].shape[1]
    plen = nz * nx * 2 * HALF
    keys = plen + ROWS
    wide = GROUP * E
    bf16, f32 = jnp.bfloat16, jnp.float32
    assert ny == nz == nx
    n = nx
    vmem = pltpu.VMEM
    hbm = pl.BlockSpec(memory_space=pl.ANY)
    dma = pltpu.SemaphoreType.DMA
    scratch = [
        vmem((depth, KVH * E), bf16),
        vmem((depth, KVH * E), bf16),
        vmem((HALF, depth), bf16),
        vmem((2, ROWS, G * wide), bf16),
        vmem((2, ROWS, G * wide), bf16),
        vmem((2, 2, ROWS, G * E), bf16),
        vmem((8, 128), jnp.int32),
        vmem((8, 128), jnp.int32),
        pltpu.SMEM((8, 128), jnp.int32),
        pltpu.SMEM((1,), jnp.int32),
        pltpu.SMEM((1, 2), jnp.int32),
        vmem((2, G, 2, HALF, E), bf16),
        vmem((G, 2, n, n, 2, HALF, E), bf16),
    ]
    scratch += [vmem((n, n, n, 2, HALF, E), bf16)] * 4
    scratch += [
        vmem((G, 2, keys, 2 * E), bf16),
        vmem((G, 2, keys, 2 * E), bf16),
        vmem((G, 2, wide, 2 * E), bf16),
        vmem((G, 2, wide, 2 * E), bf16),
        vmem((2, keys, wide), f32),
        vmem((2, keys, wide), f32),
        vmem((2, keys, wide), bf16),
        vmem((G, 2, keys, wide), bf16),
        vmem((2, keys, 2 * E), f32),
        vmem((G, 2, n, n, n, 2, HALF, E), bf16),
        vmem((G, 2, 2, n - 1, n, n, HALF, E), bf16),
        vmem((G, 2, 2, n, n, HALF, E), bf16),
        vmem((G, 2, 2, n * n - 1, HALF, E), bf16),
        vmem((G, 2, 2, HALF, E), bf16),
        vmem((G, 2, 2, HALF, E), bf16),
        vmem((depth, 2 * E), bf16),
        vmem((HALF, depth), f32),
        vmem((HALF, depth), bf16),
        vmem((2, ROWS, G * wide), bf16),
        vmem((2, 2, ROWS, G * E), bf16),
        dma((2, 2)),
        dma((8,)),
        dma((16,)),
        dma((16,)),
        dma((1,)),
        dma((G,)),
        dma((1,)),
        dma((2 * G,)),
        dma((2,)),
        dma((2, 2 * G)),
        dma((5,)),
    ]
    shape = jax.ShapeDtypeStruct
    results = (
        shape((ROWS, KVH * wide), bf16),
        shape((ROWS, KVH * E), bf16),
        shape((ROWS, KVH * E), bf16),
        shape((HALF, depth), bf16),
    )
    made = pl.pallas_call(
        functools.partial(kernel, dims),
        out_shape=results,
        in_specs=[hbm] * 9,
        out_specs=(hbm,) * 4,
        scratch_shapes=scratch,
        compiler_params=pltpu.CompilerParams(
            collective_id=0, has_side_effects=True, vmem_limit_bytes=56 * 1024 * 1024
        ),
    )(*arrays)
    return pl.pallas_call(
        hand_over,
        out_shape=results,
        in_specs=[hbm] * 4,
        out_specs=(hbm,) * 4,
        scratch_shapes=[vmem(r.shape, r.dtype) for r in results] + [dma((4,)), dma((4,))],
    )(*made)


def solution(mesh):
    ny = mesh.shape["prompt"]
    chips = mesh.shape["resp"] // 2
    nx = round(chips**0.5)
    dims = (ny, chips // nx, nx)
    rows = P(("prompt", "resp"), None)
    return jax.shard_map(
        functools.partial(per_device, dims),
        mesh=mesh,
        in_specs=(rows, P(), P(), rows, rows, rows, rows, P(("prompt", "resp")), rows),
        out_specs=(rows, rows, rows, rows),
        check_vma=False,
    )
```

```python
import functools

import jax
import jax.numpy as jnp
from jax import lax
from jax.experimental import pallas as pl
from jax.experimental.pallas import tpu as pltpu
from jax.sharding import PartitionSpec as P

MESH = pl.DeviceIdType.MESH
E = 128
KVH = 4
G = 2
GROUP = 5
ROWS = 128
HALF = 16
SCALE = E ** (-0.5)
LOG2E = 1.4426950408889634
RING = (((0, 1), (2, 0)), ((1, 2), (0, 2)))


def kernel(
    dims,
    prompt_rows,
    key_weight,
    value_weight,
    queries,
    own_keys,
    own_values,
    out_grad,
    first_length,
    resp_prompt,
    query_grad,
    key_grad,
    value_grad,
    prompt_grad,
    wk,
    wv,
    rows,
    q_in,
    g_in,
    own_in,
    scal_out,
    scal_in,
    scal,
    scal_first,
    scal_pair,
    stage,
    planes,
    kv_00,
    kv_01,
    kv_10,
    kv_11,
    keys_ab,
    values_ab,
    q_ab,
    g_ab,
    probs,
    dprobs,
    probs_t,
    dscores_t,
    parts,
    contrib,
    recv1,
    acc1,
    recv2,
    share,
    final,
    w_last,
    prompt_sum,
    prompt_out,
    dq_out,
    own_out,
    w_sem,
    in_sem,
    x_send,
    x_recv,
    hop_send,
    hop_recv,
    plane_send,
    plane_recv,
    ring_send,
    ring_recv,
    out_sem,
):
    kv = ((kv_00, kv_01), (kv_10, kv_11))
    n = dims[0]
    prompts = n
    plen = n * n * 2 * HALF
    depth = key_weight.shape[0]
    kcols = G * E
    qcols = G * GROUP * E
    r_index = lax.axis_index("resp")
    core = lax.rem(r_index, 2)
    chip = lax.div(r_index, 2)
    place = (lax.axis_index("prompt"), lax.div(chip, n), lax.rem(chip, n))
    other = 1 - core
    even = core == 0
    turned = (place[1], place[2], place[0])
    me = tuple(jnp.where(even, a, b) for a, b in zip(place, turned))
    partner_me = tuple(jnp.where(even, b, a) for a, b in zip(place, turned))

    near = [[lax.rem(me[d] + off, n) for off in range(n)] for d in range(3)]
    weight_y = (jnp.where(even, 1, 0), 0, jnp.where(even, 0, 1))
    weight_r = (jnp.where(even, 0, 2 * n), jnp.where(even, 2 * n, 2), jnp.where(even, 2, 0))
    add_y = [[near[d][off] * weight_y[d] for off in range(n)] for d in range(3)]
    add_r = [[near[d][off] * weight_r[d] for off in range(n)] for d in range(3)]

    def peer(*moves):
        off = [0, 0, 0]
        for dim, by in moves:
            off[dim] = by
        y = add_y[0][off[0]] + add_y[2][off[2]]
        r = add_r[0][off[0]] + add_r[1][off[1]] + add_r[2][off[2]] + core
        return (y, r)

    partner = (place[0], chip * 2 + other)

    steps = 2
    span = depth // steps
    mine_k = pl.ds(pl.multiple_of(core * kcols, kcols), kcols)
    theirs_k = pl.ds(pl.multiple_of(other * kcols, kcols), kcols)
    mine_q = pl.ds(pl.multiple_of(core * qcols, E), qcols)
    theirs_q = pl.ds(pl.multiple_of(other * qcols, E), qcols)

    rows_copy = pltpu.make_async_copy(prompt_rows, rows, in_sem.at[0])
    rows_copy.start()
    w_copies = {}
    for t, (src, dst) in enumerate(((key_weight, wk), (value_weight, wv))):
        for s in range(steps):
            at = pl.ds(s * span, span)
            w_copies[t, s] = pltpu.make_async_copy(src.at[at], dst.at[at], w_sem.at[t, s])
            w_copies[t, s].start()
    local = [
        pltpu.make_async_copy(own_keys.at[:, mine_k], own_in.at[0, 0], in_sem.at[1]),
        pltpu.make_async_copy(own_values.at[:, mine_k], own_in.at[0, 1], in_sem.at[2]),
        pltpu.make_async_copy(queries.at[:, mine_q], q_in.at[0], in_sem.at[3]),
        pltpu.make_async_copy(out_grad.at[:, mine_q], g_in.at[0], in_sem.at[4]),
    ]

    barrier = pltpu.get_barrier_semaphore()
    pl.semaphore_signal(barrier, inc=1, device_id=partner, device_id_type=MESH)
    greeted = [((d, off),) for d in range(3) for off in range(1, n)]
    greeted += [((d, i), (e, j)) for d in range(3) for e in range(d + 1, 3) for i in range(1, n) for j in range(1, n)]
    for moves in greeted:
        pl.semaphore_signal(barrier, inc=1, device_id=peer(*moves), device_id_type=MESH)
    scal_copies = [
        pltpu.make_async_copy(first_length, scal_first, in_sem.at[6]),
        pltpu.make_async_copy(resp_prompt, scal_pair, in_sem.at[7]),
    ]
    for c in scal_copies + local:
        c.start()

    for c in scal_copies:
        c.wait()
    l_mine = scal_first[0]
    a_mine = scal_pair[0, 0]
    b_mine = scal_pair[0, 1]
    lane8 = lax.broadcasted_iota(jnp.int32, (8, 128), 1)
    scal_out[...] = jnp.where(lane8 == 0, l_mine, jnp.where(lane8 == 1, a_mine, b_mine))
    rows_copy.wait()
    for t, weight in ((0, wk), (1, wv)):
        total = jnp.zeros((HALF, KVH * E), jnp.float32)
        for s in range(steps):
            w_copies[t, s].wait()
            at = slice(s * span, (s + 1) * span)
            total = total + jnp.dot(rows[:, at], weight[at, :], preferred_element_type=jnp.float32)
        total = total.astype(jnp.bfloat16)
        for head in range(KVH):
            stage[head // G, head % G, t] = total[:, head * E : (head + 1) * E]

    def plane_of(piece):
        return [d for d in range(3) if d != RING[piece[0]][piece[1]][piece[2]]]

    def plane_place(g, t, at):
        zero, one = plane_of((g, t, 0)), plane_of((g, t, 1))
        return tuple(jnp.where(even, at[i], at[j]) for i, j in zip(zero, one))

    heads = [(g, t) for g in range(G) for t in range(2)]
    for g, t in heads:
        a, b = plane_place(g, t, me)
        planes[g, t, core, a, b] = stage[core, g, t]

    pl.semaphore_wait(barrier, len(greeted) + 1)

    def swap(src, dst, index):
        c = pltpu.make_async_remote_copy(
            src_ref=src, dst_ref=dst, send_sem=x_send.at[index], recv_sem=x_recv.at[index],
            device_id=partner, device_id_type=MESH,
        )
        c.start()
        return c

    kv_swaps = []
    for g, t in heads:
        a, b = plane_place(g, t, partner_me)
        kv_swaps.append(swap(stage.at[other, g, t], planes.at[g, t, core, a, b], g * 2 + t))

    def remote(src, dst, sems, to):
        return pltpu.make_async_remote_copy(
            src_ref=src, dst_ref=dst, send_sem=sems[0], recv_sem=sems[1], device_id=to, device_id_type=MESH
        )

    def hop_sems(g, t):
        return hop_send.at[0], hop_recv.at[g * 2 + t]

    def plane_sems(g, t):
        return plane_send.at[0], plane_recv.at[g * 2 + t]

    def ring_sems(phase, g, t):
        return ring_send.at[phase], ring_recv.at[phase, g * 2 + t]

    def hop_arrived(g, t):
        remote(recv2.at[g, t], recv2.at[g, t], hop_sems(g, t), partner).wait_recv()

    def plane_arrived(g, t):
        remote(recv2.at[g, t], recv2.at[g, t], plane_sems(g, t), partner).wait_recv()

    def ring_arrived(phase, g, t):
        remote(recv1.at[g, t], recv1.at[g, t], ring_sems(phase, g, t), partner).wait_recv()

    beyond = [(i, j) for i in range(n) for j in range(n) if i + j > 0]

    def gather_plane(g, t):
        for h in range(2):
            a, b = plane_of((g, t, h))
            block = planes.at[g, t, h, me[a], me[b]]
            for i, j in beyond:
                remote(block, block, hop_sems(g, t), peer((a, i), (b, j))).start()

    def gather_ring(g, t, h):
        c = RING[g][t][h]
        index = tuple(me[d] if d == c else slice(None) for d in range(3)) + (h,)
        for off in range(1, n):
            remote(planes.at[g, t, h], kv[g][t].at[index], ring_sems(0, g, t), peer((c, off))).start()
        kv[g][t][index] = planes[g, t, h]

    for g, t in heads:
        kv_swaps[g * 2 + t].wait_recv()
        gather_plane(g, t)
    scal_swap = swap(scal_out, scal_in, 4)
    q_swap = swap(queries.at[:, theirs_q], q_in.at[1], 5)
    g_swap = swap(out_grad.at[:, theirs_q], g_in.at[1], 6)
    own_swaps = [
        swap(own_keys.at[:, theirs_k], own_in.at[1, 0], 7),
        swap(own_values.at[:, theirs_k], own_in.at[1, 1], 8),
    ]
    scal_swap.wait_recv()
    to_smem = pltpu.make_async_copy(scal_in, scal, in_sem.at[5])
    to_smem.start()
    to_smem.wait()
    first = (l_mine, scal[0, 0])
    prompt_a = (a_mine, scal[0, 1])
    prompt_b = (b_mine, scal[0, 2])
    for c in local:
        c.wait()
    for c in own_swaps:
        c.wait_recv()
    q_swap.wait_recv()
    g_swap.wait_recv()

    sub_j = lax.broadcasted_iota(jnp.int32, (ROWS, E), 0)
    lane_i = lax.broadcasted_iota(jnp.int32, (ROWS, E), 1)
    lane_1 = lax.broadcasted_iota(jnp.int32, (1, E), 1)
    half_1, half_2 = slice(0, E), slice(E, 2 * E)

    def prepare(g, d):
        in_a = jnp.where(sub_j < first[d], 1.0, 0.0).astype(jnp.bfloat16)
        in_b = jnp.where(sub_j < first[d], 0.0, 1.0).astype(jnp.bfloat16)
        for h in range(GROUP):
            cols = slice((g * GROUP + h) * E, (g * GROUP + h + 1) * E)
            at = slice(h * E, (h + 1) * E)
            for src, dst in ((q_in, q_ab), (g_in, g_ab)):
                value = src[d, :, cols]
                dst[g, d, at, half_1] = value * in_a
                dst[g, d, at, half_2] = value * in_b
        for t, dst in ((0, keys_ab), (1, values_ab)):
            for cols in (half_1, half_2):
                dst[g, d, plen:, cols] = own_in[d, t, :, g * E : (g + 1) * E]

    def fill(g, t, dst):
        def along(axis):
            for d in range(2):
                for cols, prompt in ((half_1, prompt_a[d]), (half_2, prompt_b[d])):
                    block = kv[g][t][prompt] if axis == 0 else kv[g][t][:, :, prompt]
                    dst[g, d, :plen, cols] = block.reshape(plen, E)

        pl.when(even)(lambda: along(0))
        pl.when(core == 1)(lambda: along(2))

    both = (((1,), (1,)), ((), ()))

    def scores(g, d):
        probs[d] = lax.dot_general(keys_ab[g, d], q_ab[g, d], both, preferred_element_type=jnp.float32)

    def probabilities(g, d):
        boundary = first[d]
        seen = (sub_j <= lane_i) & ((sub_j < boundary) == (lane_i < boundary))
        for h in range(GROUP):
            at = slice(h * E, (h + 1) * E)
            s_pre = probs[d, :plen, at]
            s_own = jnp.where(seen, probs[d, plen:, at], -jnp.inf)
            top = jnp.maximum(jnp.max(s_pre, axis=0, keepdims=True), jnp.max(s_own, axis=0, keepdims=True))
            e_pre = jnp.exp2((s_pre - top) * (SCALE * LOG2E))
            e_own = jnp.exp2((s_own - top) * (SCALE * LOG2E))
            total = jnp.sum(e_pre, axis=0, keepdims=True) + jnp.sum(e_own, axis=0, keepdims=True)
            inverse = 1.0 / total
            p_pre = e_pre * inverse
            p_own = e_own * inverse
            probs[d, :plen, at] = p_pre
            probs[d, plen:, at] = p_own
            probs_t[d, :plen, at] = p_pre.astype(jnp.bfloat16)
            probs_t[d, plen:, at] = p_own.astype(jnp.bfloat16)
        parts[d] = jnp.dot(probs_t[d], g_ab[g, d], preferred_element_type=jnp.float32)
        own_out[d, 1, :, g * E : (g + 1) * E] = (parts[d, plen:, half_1] + parts[d, plen:, half_2]).astype(jnp.bfloat16)

    def prob_gradients(g, d):
        dprobs[d] = lax.dot_general(values_ab[g, d], g_ab[g, d], both, preferred_element_type=jnp.float32)

    def score_gradients(g, d):
        for h in range(GROUP):
            at = slice(h * E, (h + 1) * E)
            dp = dprobs[d, :, at]
            delta = jnp.sum(probs_t[d, :, at].astype(jnp.float32) * dp, axis=0, keepdims=True)
            dscores_t[g, d, :, at] = (probs[d, :, at] * (dp - delta)).astype(jnp.bfloat16)
        parts[d] = jnp.dot(dscores_t[g, d], q_ab[g, d], preferred_element_type=jnp.float32)
        own_out[d, 0, :, g * E : (g + 1) * E] = (
            (parts[d, plen:, half_1] + parts[d, plen:, half_2]) * SCALE
        ).astype(jnp.bfloat16)

    def query_gradients(g, d):
        dq_t = jnp.dot(keys_ab[g, d].T, dscores_t[g, d], preferred_element_type=jnp.float32)
        for h in range(GROUP):
            at = slice(h * E, (h + 1) * E)
            picked = jnp.where(lane_1 < first[d], dq_t[:E, at], dq_t[E:, at]) * SCALE
            cols = slice((g * GROUP + h) * E, (g * GROUP + h + 1) * E)
            dq_out[d, :, cols] = picked.T.astype(jnp.bfloat16)

    def contribute(g, t):
        unit = SCALE if t == 0 else 1.0

        def along(axis):
            for p in range(prompts):
                total = None
                for d in range(2):
                    for cols, prompt in ((half_1, prompt_a[d]), (half_2, prompt_b[d])):
                        gate = jnp.where(prompt == p, unit, 0.0).astype(jnp.float32)
                        term = parts[d, :plen, cols] * gate
                        total = term if total is None else total + term
                block = total.astype(jnp.bfloat16).reshape(n, n, 2, HALF, E)
                if axis == 0:
                    contrib[g, t, p] = block
                else:
                    contrib[g, t, :, :, p] = block

        pl.when(even)(lambda: along(0))
        pl.when(core == 1)(lambda: along(2))

    def scatter_ring(g, t, h):
        c = RING[g][t][h]
        for off in range(1, n):
            index = tuple(near[d][off] if d == c else slice(None) for d in range(3))
            remote(
                contrib.at[(g, t) + index + (h,)], recv1.at[g, t, h, off - 1], ring_sems(1, g, t), peer((c, off))
            ).start()

    def scatter_plane(g, t):
        ring_arrived(1, g, t)
        for h in range(2):
            c = RING[g][t][h]
            index = tuple(me[d] if d == c else slice(None) for d in range(3))
            total = contrib[(g, t) + index + (h,)].astype(jnp.float32)
            for off in range(1, n):
                total = total + recv1[g, t, h, off - 1].astype(jnp.float32)
            acc1[g, t, h] = total.astype(jnp.bfloat16)
            a, b = plane_of((g, t, h))
            for i, j in beyond:
                remote(
                    acc1.at[g, t, h, near[a][i], near[b][j]], recv2.at[g, t, h, i * n + j - 1], plane_sems(g, t),
                    peer((a, i), (b, j)),
                ).start()

    def scatter_end(g, t):
        plane_arrived(g, t)
        for h in range(2):
            a, b = plane_of((g, t, h))
            total = acc1[g, t, h, me[a], me[b]].astype(jnp.float32)
            total = total + jnp.sum(recv2[g, t, h].astype(jnp.float32), axis=0)
            share[g, t, h] = total.astype(jnp.bfloat16)
        c = swap(share.at[g, t, other], final.at[g, t, core], 12 + g * 2 + t)
        final[g, t, core] = share[g, t, core]
        return c

    for g in range(G):
        for d in range(2):
            prepare(g, d)
    for g, t in heads:
        hop_arrived(g, t)
        for h in range(2):
            gather_ring(g, t, h)

    for g in range(G):
        ring_arrived(0, g, 0)
        fill(g, 0, keys_ab)
        for d in range(2):
            scores(g, d)
        for d in range(2):
            probabilities(g, d)
        contribute(g, 1)
        for h in range(2):
            scatter_ring(g, 1, h)
        ring_arrived(0, g, 1)
        fill(g, 1, values_ab)
        for d in range(2):
            prob_gradients(g, d)
        for d in range(2):
            score_gradients(g, d)
        contribute(g, 0)
        for h in range(2):
            scatter_ring(g, 0, h)

    for d in range(2):
        query_gradients(0, d)
    for t in (1, 0):
        scatter_plane(0, t)
    for d in range(2):
        query_gradients(1, d)
    for t in (1, 0):
        scatter_plane(1, t)
    home = [
        pltpu.make_async_copy(dq_out.at[0], query_grad.at[:, mine_q], out_sem.at[0]),
        pltpu.make_async_copy(own_out.at[0, 0], key_grad.at[:, mine_k], out_sem.at[1]),
        pltpu.make_async_copy(own_out.at[0, 1], value_grad.at[:, mine_k], out_sem.at[2]),
    ]
    for c in home:
        c.start()
    away = [
        swap(dq_out.at[1], query_grad.at[:, mine_q], 9),
        swap(own_out.at[1, 0], key_grad.at[:, mine_k], 10),
        swap(own_out.at[1, 1], value_grad.at[:, mine_k], 11),
    ]

    tile = 512
    tiles = [slice(i * tile, (i + 1) * tile) for i in range(depth // tile)]

    def last_product(g, t, at):
        weight = (wk, wv)[t]
        total = None
        for c in range(2):
            head = slice((c * G + g) * E, (c * G + g + 1) * E)
            term = lax.dot_general(final[g, t, c], weight[at, head], both, preferred_element_type=jnp.float32)
            total = term if total is None else total + term
        return total

    for c in range(2):
        w_last[:, c * E : (c + 1) * E] = wk[:, (c * G + 1) * E : (c * G + 2) * E]

    final_swaps = [scatter_end(0, 1), scatter_end(0, 0)]
    for c in final_swaps:
        c.wait_recv()
    for at in tiles:
        prompt_sum[:, at] = last_product(0, 1, at) + last_product(0, 0, at)
    final_swaps.append(scatter_end(1, 1))
    final_swaps[2].wait_recv()
    for at in tiles:
        prompt_sum[:, at] = prompt_sum[:, at] + last_product(1, 1, at)
    final_swaps.append(scatter_end(1, 0))
    final_swaps[3].wait_recv()
    x_last = jnp.concatenate([final[1, 0, 0], final[1, 0, 1]], axis=1)
    prompt_copies = []
    parted = len(tiles) // 2
    for k, group in enumerate((tiles[:parted], tiles[parted:])):
        for at in group:
            total = lax.dot_general(x_last, w_last[at, :], both, preferred_element_type=jnp.float32)
            prompt_out[:, at] = (prompt_sum[:, at] + total).astype(jnp.bfloat16)
        whole = slice(group[0].start, group[-1].stop)
        prompt_copies.append(
            pltpu.make_async_copy(prompt_out.at[:, whole], prompt_grad.at[:, whole], out_sem.at[3 + k])
        )
        prompt_copies[k].start()

    for phase in range(2):
        remote(recv1, recv1, ring_sems(phase, 0, 0), partner).wait_send()
    remote(recv2, recv2, hop_sems(0, 0), partner).wait_send()
    remote(recv2, recv2, plane_sems(0, 0), partner).wait_send()
    for c in kv_swaps + own_swaps + away + [scal_swap, q_swap, g_swap] + final_swaps:
        c.wait_send()
    for c in home + prompt_copies:
        c.wait()
    for c in away:
        c.wait_recv()


def hand_over(*refs):
    sources, results, buffers, arrive, leave = refs[:4], refs[4:8], refs[8:12], refs[12], refs[13]
    inward = [pltpu.make_async_copy(a, b, arrive.at[i]) for i, (a, b) in enumerate(zip(sources, buffers))]
    outward = [pltpu.make_async_copy(b, c, leave.at[i]) for i, (b, c) in enumerate(zip(buffers, results))]
    for c in inward:
        c.start()
    for c, after in zip(inward, outward):
        c.wait()
        after.start()
    for c in outward:
        c.wait()


def per_device(dims, *arrays):
    ny, nz, nx = dims
    depth = arrays[0].shape[1]
    plen = nz * nx * 2 * HALF
    keys = plen + ROWS
    wide = GROUP * E
    bf16, f32 = jnp.bfloat16, jnp.float32
    assert ny == nz == nx
    n = nx
    vmem = pltpu.VMEM
    hbm = pl.BlockSpec(memory_space=pl.ANY)
    dma = pltpu.SemaphoreType.DMA
    scratch = [
        vmem((depth, KVH * E), bf16),
        vmem((depth, KVH * E), bf16),
        vmem((HALF, depth), bf16),
        vmem((2, ROWS, G * wide), bf16),
        vmem((2, ROWS, G * wide), bf16),
        vmem((2, 2, ROWS, G * E), bf16),
        vmem((8, 128), jnp.int32),
        vmem((8, 128), jnp.int32),
        pltpu.SMEM((8, 128), jnp.int32),
        pltpu.SMEM((1,), jnp.int32),
        pltpu.SMEM((1, 2), jnp.int32),
        vmem((2, G, 2, HALF, E), bf16),
        vmem((G, 2, 2, n, n, HALF, E), bf16),
    ]
    scratch += [vmem((n, n, n, 2, HALF, E), bf16)] * 4
    scratch += [
        vmem((G, 2, keys, 2 * E), bf16),
        vmem((G, 2, keys, 2 * E), bf16),
        vmem((G, 2, wide, 2 * E), bf16),
        vmem((G, 2, wide, 2 * E), bf16),
        vmem((2, keys, wide), f32),
        vmem((2, keys, wide), f32),
        vmem((2, keys, wide), bf16),
        vmem((G, 2, keys, wide), bf16),
        vmem((2, keys, 2 * E), f32),
        vmem((G, 2, n, n, n, 2, HALF, E), bf16),
        vmem((G, 2, 2, n - 1, n, n, HALF, E), bf16),
        vmem((G, 2, 2, n, n, HALF, E), bf16),
        vmem((G, 2, 2, n * n - 1, HALF, E), bf16),
        vmem((G, 2, 2, HALF, E), bf16),
        vmem((G, 2, 2, HALF, E), bf16),
        vmem((depth, 2 * E), bf16),
        vmem((HALF, depth), f32),
        vmem((HALF, depth), bf16),
        vmem((2, ROWS, G * wide), bf16),
        vmem((2, 2, ROWS, G * E), bf16),
        dma((2, 2)),
        dma((8,)),
        dma((16,)),
        dma((16,)),
        dma((1,)),
        dma((2 * G,)),
        dma((1,)),
        dma((2 * G,)),
        dma((2,)),
        dma((2, 2 * G)),
        dma((5,)),
    ]
    shape = jax.ShapeDtypeStruct
    results = (
        shape((ROWS, KVH * wide), bf16),
        shape((ROWS, KVH * E), bf16),
        shape((ROWS, KVH * E), bf16),
        shape((HALF, depth), bf16),
    )
    made = pl.pallas_call(
        functools.partial(kernel, dims),
        out_shape=results,
        in_specs=[hbm] * 9,
        out_specs=(hbm,) * 4,
        scratch_shapes=scratch,
        compiler_params=pltpu.CompilerParams(
            collective_id=0, has_side_effects=True, vmem_limit_bytes=56 * 1024 * 1024
        ),
    )(*arrays)
    return pl.pallas_call(
        hand_over,
        out_shape=results,
        in_specs=[hbm] * 4,
        out_specs=(hbm,) * 4,
        scratch_shapes=[vmem(r.shape, r.dtype) for r in results] + [dma((4,)), dma((4,))],
    )(*made)


def solution(mesh):
    ny = mesh.shape["prompt"]
    chips = mesh.shape["resp"] // 2
    nx = round(chips**0.5)
    dims = (ny, chips // nx, nx)
    rows = P(("prompt", "resp"), None)
    return jax.shard_map(
        functools.partial(per_device, dims),
        mesh=mesh,
        in_specs=(rows, P(), P(), rows, rows, rows, rows, P(("prompt", "resp")), rows),
        out_specs=(rows, rows, rows, rows),
        check_vma=False,
    )
```

```python
import functools

import jax
import jax.numpy as jnp
from jax import lax
from jax.experimental import pallas as pl
from jax.experimental.pallas import tpu as pltpu
from jax.sharding import PartitionSpec as P

MESH = pl.DeviceIdType.MESH
E = 128
KVH = 4
G = 2
GROUP = 5
ROWS = 128
HALF = 16
SCALE = E ** (-0.5)
LOG2E = 1.4426950408889634
RING = (((0, 1), (2, 0)), ((1, 2), (0, 2)))


def kernel(
    dims,
    prompt_rows,
    key_weight,
    value_weight,
    queries,
    own_keys,
    own_values,
    out_grad,
    first_length,
    resp_prompt,
    query_grad,
    key_grad,
    value_grad,
    prompt_grad,
    wk,
    wv,
    rows,
    q_in,
    g_in,
    own_in,
    scal_out,
    scal_in,
    scal,
    scal_first,
    scal_pair,
    stage,
    planes,
    kv_00,
    kv_01,
    kv_10,
    kv_11,
    keys_ab,
    values_ab,
    q_ab,
    g_ab,
    probs,
    dprobs,
    probs_t,
    dscores_t,
    parts,
    contrib,
    recv1,
    acc1,
    recv2,
    share,
    final,
    w_last,
    prompt_sum,
    prompt_out,
    dq_out,
    own_out,
    w_sem,
    in_sem,
    x_send,
    x_recv,
    hop_send,
    hop_recv,
    plane_send,
    plane_recv,
    ring_send,
    ring_recv,
    out_sem,
):
    kv = ((kv_00, kv_01), (kv_10, kv_11))
    n = dims[0]
    prompts = n
    plen = n * n * 2 * HALF
    depth = key_weight.shape[0]
    kcols = G * E
    qcols = G * GROUP * E
    r_index = lax.axis_index("resp")
    core = lax.rem(r_index, 2)
    chip = lax.div(r_index, 2)
    place = (lax.axis_index("prompt"), lax.div(chip, n), lax.rem(chip, n))
    other = 1 - core
    even = core == 0
    turned = (place[1], place[2], place[0])
    me = tuple(jnp.where(even, a, b) for a, b in zip(place, turned))
    partner_me = tuple(jnp.where(even, b, a) for a, b in zip(place, turned))

    near = [[lax.rem(me[d] + off, n) for off in range(n)] for d in range(3)]
    weight_y = (jnp.where(even, 1, 0), 0, jnp.where(even, 0, 1))
    weight_r = (jnp.where(even, 0, 2 * n), jnp.where(even, 2 * n, 2), jnp.where(even, 2, 0))
    add_y = [[near[d][off] * weight_y[d] for off in range(n)] for d in range(3)]
    add_r = [[near[d][off] * weight_r[d] for off in range(n)] for d in range(3)]

    def peer(*moves):
        off = [0, 0, 0]
        for dim, by in moves:
            off[dim] = by
        y = add_y[0][off[0]] + add_y[2][off[2]]
        r = add_r[0][off[0]] + add_r[1][off[1]] + add_r[2][off[2]] + core
        return (y, r)

    partner = (place[0], chip * 2 + other)

    steps = 2
    span = depth // steps
    mine_k = pl.ds(pl.multiple_of(core * kcols, kcols), kcols)
    theirs_k = pl.ds(pl.multiple_of(other * kcols, kcols), kcols)
    mine_q = pl.ds(pl.multiple_of(core * qcols, E), qcols)
    theirs_q = pl.ds(pl.multiple_of(other * qcols, E), qcols)

    rows_copy = pltpu.make_async_copy(prompt_rows, rows, in_sem.at[0])
    rows_copy.start()
    w_copies = {}
    for t, (src, dst) in enumerate(((key_weight, wk), (value_weight, wv))):
        for s in range(steps):
            at = pl.ds(s * span, span)
            w_copies[t, s] = pltpu.make_async_copy(src.at[at], dst.at[at], w_sem.at[t, s])
            w_copies[t, s].start()
    local = [
        pltpu.make_async_copy(own_keys.at[:, mine_k], own_in.at[0, 0], in_sem.at[1]),
        pltpu.make_async_copy(own_values.at[:, mine_k], own_in.at[0, 1], in_sem.at[2]),
        pltpu.make_async_copy(queries.at[:, mine_q], q_in.at[0], in_sem.at[3]),
        pltpu.make_async_copy(out_grad.at[:, mine_q], g_in.at[0], in_sem.at[4]),
    ]

    barrier = pltpu.get_barrier_semaphore()
    pl.semaphore_signal(barrier, inc=1, device_id=partner, device_id_type=MESH)
    greeted = [((d, off),) for d in range(3) for off in range(1, n)]
    greeted += [((d, i), (e, j)) for d in range(3) for e in range(d + 1, 3) for i in range(1, n) for j in range(1, n)]
    for moves in greeted:
        pl.semaphore_signal(barrier, inc=1, device_id=peer(*moves), device_id_type=MESH)
    scal_copies = [
        pltpu.make_async_copy(first_length, scal_first, in_sem.at[6]),
        pltpu.make_async_copy(resp_prompt, scal_pair, in_sem.at[7]),
    ]
    for c in scal_copies + local:
        c.start()

    for c in scal_copies:
        c.wait()
    l_mine = scal_first[0]
    a_mine = scal_pair[0, 0]
    b_mine = scal_pair[0, 1]
    lane8 = lax.broadcasted_iota(jnp.int32, (8, 128), 1)
    scal_out[...] = jnp.where(lane8 == 0, l_mine, jnp.where(lane8 == 1, a_mine, b_mine))
    rows_copy.wait()
    for t, weight in ((0, wk), (1, wv)):
        total = jnp.zeros((HALF, KVH * E), jnp.float32)
        for s in range(steps):
            w_copies[t, s].wait()
            at = slice(s * span, (s + 1) * span)
            total = total + jnp.dot(rows[:, at], weight[at, :], preferred_element_type=jnp.float32)
        total = total.astype(jnp.bfloat16)
        for head in range(KVH):
            stage[head // G, head % G, t] = total[:, head * E : (head + 1) * E]

    def plane_of(piece):
        return [d for d in range(3) if d != RING[piece[0]][piece[1]][piece[2]]]

    def plane_place(g, t, at):
        zero, one = plane_of((g, t, 0)), plane_of((g, t, 1))
        return tuple(jnp.where(even, at[i], at[j]) for i, j in zip(zero, one))

    heads = [(g, t) for g in range(G) for t in range(2)]
    for g, t in heads:
        a, b = plane_place(g, t, me)
        planes[g, t, core, a, b] = stage[core, g, t]

    pl.semaphore_wait(barrier, len(greeted) + 1)

    def swap(src, dst, index):
        c = pltpu.make_async_remote_copy(
            src_ref=src, dst_ref=dst, send_sem=x_send.at[index], recv_sem=x_recv.at[index],
            device_id=partner, device_id_type=MESH,
        )
        c.start()
        return c

    kv_swaps = []
    for g, t in heads:
        a, b = plane_place(g, t, partner_me)
        kv_swaps.append(swap(stage.at[other, g, t], planes.at[g, t, core, a, b], g * 2 + t))

    def remote(src, dst, sems, to):
        return pltpu.make_async_remote_copy(
            src_ref=src, dst_ref=dst, send_sem=sems[0], recv_sem=sems[1], device_id=to, device_id_type=MESH
        )

    def hop_sems(g, t):
        return hop_send.at[0], hop_recv.at[g * 2 + t]

    def plane_sems(g, t):
        return plane_send.at[0], plane_recv.at[g * 2 + t]

    def ring_sems(phase, g, t):
        return ring_send.at[phase], ring_recv.at[phase, g * 2 + t]

    def hop_arrived(g, t):
        remote(recv2.at[g, t], recv2.at[g, t], hop_sems(g, t), partner).wait_recv()

    def plane_arrived(g, t):
        remote(recv2.at[g, t], recv2.at[g, t], plane_sems(g, t), partner).wait_recv()

    def ring_arrived(phase, g, t):
        remote(recv1.at[g, t], recv1.at[g, t], ring_sems(phase, g, t), partner).wait_recv()

    beyond = [(i, j) for i in range(n) for j in range(n) if i + j > 0]

    def gather_plane(g, t):
        for h in range(2):
            a, b = plane_of((g, t, h))
            block = planes.at[g, t, h, me[a], me[b]]
            for i, j in beyond:
                remote(block, block, hop_sems(g, t), peer((a, i), (b, j))).start()

    def gather_ring(g, t, h):
        c = RING[g][t][h]
        index = tuple(me[d] if d == c else slice(None) for d in range(3)) + (h,)
        for off in range(1, n):
            remote(planes.at[g, t, h], kv[g][t].at[index], ring_sems(0, g, t), peer((c, off))).start()
        kv[g][t][index] = planes[g, t, h]

    for g, t in heads:
        kv_swaps[g * 2 + t].wait_recv()
        gather_plane(g, t)
    scal_swap = swap(scal_out, scal_in, 4)
    q_swap = swap(queries.at[:, theirs_q], q_in.at[1], 5)
    g_swap = swap(out_grad.at[:, theirs_q], g_in.at[1], 6)
    own_swaps = [
        swap(own_keys.at[:, theirs_k], own_in.at[1, 0], 7),
        swap(own_values.at[:, theirs_k], own_in.at[1, 1], 8),
    ]
    scal_swap.wait_recv()
    to_smem = pltpu.make_async_copy(scal_in, scal, in_sem.at[5])
    to_smem.start()
    to_smem.wait()
    first = (l_mine, scal[0, 0])
    prompt_a = (a_mine, scal[0, 1])
    prompt_b = (b_mine, scal[0, 2])
    for c in local:
        c.wait()
    for c in own_swaps:
        c.wait_recv()
    q_swap.wait_recv()
    g_swap.wait_recv()

    sub_j = lax.broadcasted_iota(jnp.int32, (ROWS, E), 0)
    lane_i = lax.broadcasted_iota(jnp.int32, (ROWS, E), 1)
    lane_1 = lax.broadcasted_iota(jnp.int32, (1, E), 1)
    half_1, half_2 = slice(0, E), slice(E, 2 * E)

    def prepare(g, d):
        in_a = jnp.where(sub_j < first[d], 1.0, 0.0).astype(jnp.bfloat16)
        in_b = jnp.where(sub_j < first[d], 0.0, 1.0).astype(jnp.bfloat16)
        for h in range(GROUP):
            cols = slice((g * GROUP + h) * E, (g * GROUP + h + 1) * E)
            at = slice(h * E, (h + 1) * E)
            for src, dst in ((q_in, q_ab), (g_in, g_ab)):
                value = src[d, :, cols]
                dst[g, d, at, half_1] = value * in_a
                dst[g, d, at, half_2] = value * in_b
        for t, dst in ((0, keys_ab), (1, values_ab)):
            for cols in (half_1, half_2):
                dst[g, d, plen:, cols] = own_in[d, t, :, g * E : (g + 1) * E]

    def fill(g, t, dst):
        def along(axis):
            for d in range(2):
                for cols, prompt in ((half_1, prompt_a[d]), (half_2, prompt_b[d])):
                    block = kv[g][t][prompt] if axis == 0 else kv[g][t][:, :, prompt]
                    dst[g, d, :plen, cols] = block.reshape(plen, E)

        pl.when(even)(lambda: along(0))
        pl.when(core == 1)(lambda: along(2))

    both = (((1,), (1,)), ((), ()))

    def scores(g, d):
        probs[d] = lax.dot_general(keys_ab[g, d], q_ab[g, d], both, preferred_element_type=jnp.float32)

    def probabilities(g, d):
        boundary = first[d]
        seen = (sub_j <= lane_i) & ((sub_j < boundary) == (lane_i < boundary))
        for h in range(GROUP):
            at = slice(h * E, (h + 1) * E)
            s_pre = probs[d, :plen, at]
            s_own = jnp.where(seen, probs[d, plen:, at], -jnp.inf)
            top = jnp.maximum(jnp.max(s_pre, axis=0, keepdims=True), jnp.max(s_own, axis=0, keepdims=True))
            e_pre = jnp.exp2((s_pre - top) * (SCALE * LOG2E))
            e_own = jnp.exp2((s_own - top) * (SCALE * LOG2E))
            total = jnp.sum(e_pre, axis=0, keepdims=True) + jnp.sum(e_own, axis=0, keepdims=True)
            inverse = 1.0 / total
            p_pre = e_pre * inverse
            p_own = e_own * inverse
            probs[d, :plen, at] = p_pre
            probs[d, plen:, at] = p_own
            probs_t[d, :plen, at] = p_pre.astype(jnp.bfloat16)
            probs_t[d, plen:, at] = p_own.astype(jnp.bfloat16)
        parts[d] = jnp.dot(probs_t[d], g_ab[g, d], preferred_element_type=jnp.float32)
        own_out[d, 1, :, g * E : (g + 1) * E] = (parts[d, plen:, half_1] + parts[d, plen:, half_2]).astype(jnp.bfloat16)

    def prob_gradients(g, d):
        dprobs[d] = lax.dot_general(values_ab[g, d], g_ab[g, d], both, preferred_element_type=jnp.float32)

    def score_gradients(g, d):
        for h in range(GROUP):
            at = slice(h * E, (h + 1) * E)
            dp = dprobs[d, :, at]
            delta = jnp.sum(probs_t[d, :, at].astype(jnp.float32) * dp, axis=0, keepdims=True)
            dscores_t[g, d, :, at] = (probs[d, :, at] * (dp - delta)).astype(jnp.bfloat16)
        parts[d] = jnp.dot(dscores_t[g, d], q_ab[g, d], preferred_element_type=jnp.float32)
        own_out[d, 0, :, g * E : (g + 1) * E] = (
            (parts[d, plen:, half_1] + parts[d, plen:, half_2]) * SCALE
        ).astype(jnp.bfloat16)

    def query_gradients(g, d):
        dq_t = jnp.dot(keys_ab[g, d].T, dscores_t[g, d], preferred_element_type=jnp.float32)
        for h in range(GROUP):
            at = slice(h * E, (h + 1) * E)
            picked = jnp.where(lane_1 < first[d], dq_t[:E, at], dq_t[E:, at]) * SCALE
            cols = slice((g * GROUP + h) * E, (g * GROUP + h + 1) * E)
            dq_out[d, :, cols] = picked.T.astype(jnp.bfloat16)

    def contribute(g, t):
        unit = SCALE if t == 0 else 1.0

        def along(axis):
            for p in range(prompts):
                total = None
                for d in range(2):
                    for cols, prompt in ((half_1, prompt_a[d]), (half_2, prompt_b[d])):
                        gate = jnp.where(prompt == p, unit, 0.0).astype(jnp.float32)
                        term = parts[d, :plen, cols] * gate
                        total = term if total is None else total + term
                block = total.astype(jnp.bfloat16).reshape(n, n, 2, HALF, E)
                if axis == 0:
                    contrib[g, t, p] = block
                else:
                    contrib[g, t, :, :, p] = block

        pl.when(even)(lambda: along(0))
        pl.when(core == 1)(lambda: along(2))

    def scatter_ring(g, t, h):
        c = RING[g][t][h]
        for off in range(1, n):
            index = tuple(near[d][off] if d == c else slice(None) for d in range(3))
            remote(
                contrib.at[(g, t) + index + (h,)], recv1.at[g, t, h, off - 1], ring_sems(1, g, t), peer((c, off))
            ).start()

    def scatter_plane(g, t):
        ring_arrived(1, g, t)
        for h in range(2):
            c = RING[g][t][h]
            index = tuple(me[d] if d == c else slice(None) for d in range(3))
            total = contrib[(g, t) + index + (h,)].astype(jnp.float32)
            for off in range(1, n):
                total = total + recv1[g, t, h, off - 1].astype(jnp.float32)
            acc1[g, t, h] = total.astype(jnp.bfloat16)
            a, b = plane_of((g, t, h))
            for i, j in beyond:
                remote(
                    acc1.at[g, t, h, near[a][i], near[b][j]], recv2.at[g, t, h, i * n + j - 1], plane_sems(g, t),
                    peer((a, i), (b, j)),
                ).start()

    def scatter_end(g, t):
        plane_arrived(g, t)
        for h in range(2):
            a, b = plane_of((g, t, h))
            total = acc1[g, t, h, me[a], me[b]].astype(jnp.float32)
            total = total + jnp.sum(recv2[g, t, h].astype(jnp.float32), axis=0)
            share[g, t, h] = total.astype(jnp.bfloat16)
        c = swap(share.at[g, t, other], final.at[g, t, core], 12 + g * 2 + t)
        final[g, t, core] = share[g, t, core]
        return c

    for g in range(G):
        for d in range(2):
            prepare(g, d)
    for g, t in heads:
        hop_arrived(g, t)
        for h in range(2):
            gather_ring(g, t, h)

    for g in range(G):
        ring_arrived(0, g, 0)
        fill(g, 0, keys_ab)
        for d in range(2):
            scores(g, d)
        for d in range(2):
            probabilities(g, d)
        contribute(g, 1)
        for h in range(2):
            scatter_ring(g, 1, h)
        ring_arrived(0, g, 1)
        fill(g, 1, values_ab)
        for d in range(2):
            prob_gradients(g, d)
        for d in range(2):
            score_gradients(g, d)
        contribute(g, 0)
        for h in range(2):
            scatter_ring(g, 0, h)

    for t in (1, 0):
        scatter_plane(0, t)
    for d in range(2):
        query_gradients(0, d)
    for d in range(2):
        query_gradients(1, d)
    for t in (1, 0):
        scatter_plane(1, t)
    home = [
        pltpu.make_async_copy(dq_out.at[0], query_grad.at[:, mine_q], out_sem.at[0]),
        pltpu.make_async_copy(own_out.at[0, 0], key_grad.at[:, mine_k], out_sem.at[1]),
        pltpu.make_async_copy(own_out.at[0, 1], value_grad.at[:, mine_k], out_sem.at[2]),
    ]
    for c in home:
        c.start()
    away = [
        swap(dq_out.at[1], query_grad.at[:, mine_q], 9),
        swap(own_out.at[1, 0], key_grad.at[:, mine_k], 10),
        swap(own_out.at[1, 1], value_grad.at[:, mine_k], 11),
    ]

    tile = 512
    tiles = [slice(i * tile, (i + 1) * tile) for i in range(depth // tile)]

    def last_product(g, t, at):
        weight = (wk, wv)[t]
        total = None
        for c in range(2):
            head = slice((c * G + g) * E, (c * G + g + 1) * E)
            term = lax.dot_general(final[g, t, c], weight[at, head], both, preferred_element_type=jnp.float32)
            total = term if total is None else total + term
        return total

    for c in range(2):
        w_last[:, c * E : (c + 1) * E] = wk[:, (c * G + 1) * E : (c * G + 2) * E]

    final_swaps = [scatter_end(0, 1), scatter_end(0, 0)]
    for c in final_swaps:
        c.wait_recv()
    for at in tiles:
        prompt_sum[:, at] = last_product(0, 1, at) + last_product(0, 0, at)
    final_swaps.append(scatter_end(1, 1))
    final_swaps[2].wait_recv()
    for at in tiles:
        prompt_sum[:, at] = prompt_sum[:, at] + last_product(1, 1, at)
    final_swaps.append(scatter_end(1, 0))
    final_swaps[3].wait_recv()
    x_last = jnp.concatenate([final[1, 0, 0], final[1, 0, 1]], axis=1)
    prompt_copies = []
    parted = len(tiles) // 2
    for k, group in enumerate((tiles[:parted], tiles[parted:])):
        for at in group:
            total = lax.dot_general(x_last, w_last[at, :], both, preferred_element_type=jnp.float32)
            prompt_out[:, at] = (prompt_sum[:, at] + total).astype(jnp.bfloat16)
        whole = slice(group[0].start, group[-1].stop)
        prompt_copies.append(
            pltpu.make_async_copy(prompt_out.at[:, whole], prompt_grad.at[:, whole], out_sem.at[3 + k])
        )
        prompt_copies[k].start()

    for phase in range(2):
        remote(recv1, recv1, ring_sems(phase, 0, 0), partner).wait_send()
    remote(recv2, recv2, hop_sems(0, 0), partner).wait_send()
    remote(recv2, recv2, plane_sems(0, 0), partner).wait_send()
    for c in kv_swaps + own_swaps + away + [scal_swap, q_swap, g_swap] + final_swaps:
        c.wait_send()
    for c in home + prompt_copies:
        c.wait()
    for c in away:
        c.wait_recv()


def hand_over(*refs):
    sources, results, buffers, arrive, leave = refs[:4], refs[4:8], refs[8:12], refs[12], refs[13]
    inward = [pltpu.make_async_copy(a, b, arrive.at[i]) for i, (a, b) in enumerate(zip(sources, buffers))]
    outward = [pltpu.make_async_copy(b, c, leave.at[i]) for i, (b, c) in enumerate(zip(buffers, results))]
    for c in inward:
        c.start()
    for c, after in zip(inward, outward):
        c.wait()
        after.start()
    for c in outward:
        c.wait()


def per_device(dims, *arrays):
    ny, nz, nx = dims
    depth = arrays[0].shape[1]
    plen = nz * nx * 2 * HALF
    keys = plen + ROWS
    wide = GROUP * E
    bf16, f32 = jnp.bfloat16, jnp.float32
    assert ny == nz == nx
    n = nx
    vmem = pltpu.VMEM
    hbm = pl.BlockSpec(memory_space=pl.ANY)
    dma = pltpu.SemaphoreType.DMA
    scratch = [
        vmem((depth, KVH * E), bf16),
        vmem((depth, KVH * E), bf16),
        vmem((HALF, depth), bf16),
        vmem((2, ROWS, G * wide), bf16),
        vmem((2, ROWS, G * wide), bf16),
        vmem((2, 2, ROWS, G * E), bf16),
        vmem((8, 128), jnp.int32),
        vmem((8, 128), jnp.int32),
        pltpu.SMEM((8, 128), jnp.int32),
        pltpu.SMEM((1,), jnp.int32),
        pltpu.SMEM((1, 2), jnp.int32),
        vmem((2, G, 2, HALF, E), bf16),
        vmem((G, 2, 2, n, n, HALF, E), bf16),
    ]
    scratch += [vmem((n, n, n, 2, HALF, E), bf16)] * 4
    scratch += [
        vmem((G, 2, keys, 2 * E), bf16),
        vmem((G, 2, keys, 2 * E), bf16),
        vmem((G, 2, wide, 2 * E), bf16),
        vmem((G, 2, wide, 2 * E), bf16),
        vmem((2, keys, wide), f32),
        vmem((2, keys, wide), f32),
        vmem((2, keys, wide), bf16),
        vmem((G, 2, keys, wide), bf16),
        vmem((2, keys, 2 * E), f32),
        vmem((G, 2, n, n, n, 2, HALF, E), bf16),
        vmem((G, 2, 2, n - 1, n, n, HALF, E), bf16),
        vmem((G, 2, 2, n, n, HALF, E), bf16),
        vmem((G, 2, 2, n * n - 1, HALF, E), bf16),
        vmem((G, 2, 2, HALF, E), bf16),
        vmem((G, 2, 2, HALF, E), bf16),
        vmem((depth, 2 * E), bf16),
        vmem((HALF, depth), f32),
        vmem((HALF, depth), bf16),
        vmem((2, ROWS, G * wide), bf16),
        vmem((2, 2, ROWS, G * E), bf16),
        dma((2, 2)),
        dma((8,)),
        dma((16,)),
        dma((16,)),
        dma((1,)),
        dma((2 * G,)),
        dma((1,)),
        dma((2 * G,)),
        dma((2,)),
        dma((2, 2 * G)),
        dma((5,)),
    ]
    shape = jax.ShapeDtypeStruct
    results = (
        shape((ROWS, KVH * wide), bf16),
        shape((ROWS, KVH * E), bf16),
        shape((ROWS, KVH * E), bf16),
        shape((HALF, depth), bf16),
    )
    made = pl.pallas_call(
        functools.partial(kernel, dims),
        out_shape=results,
        in_specs=[hbm] * 9,
        out_specs=(hbm,) * 4,
        scratch_shapes=scratch,
        compiler_params=pltpu.CompilerParams(
            collective_id=0, has_side_effects=True, vmem_limit_bytes=56 * 1024 * 1024
        ),
    )(*arrays)
    return pl.pallas_call(
        hand_over,
        out_shape=results,
        in_specs=[hbm] * 4,
        out_specs=(hbm,) * 4,
        scratch_shapes=[vmem(r.shape, r.dtype) for r in results] + [dma((4,)), dma((4,))],
    )(*made)


def solution(mesh):
    ny = mesh.shape["prompt"]
    chips = mesh.shape["resp"] // 2
    nx = round(chips**0.5)
    dims = (ny, chips // nx, nx)
    rows = P(("prompt", "resp"), None)
    return jax.shard_map(
        functools.partial(per_device, dims),
        mesh=mesh,
        in_specs=(rows, P(), P(), rows, rows, rows, rows, P(("prompt", "resp")), rows),
        out_specs=(rows, rows, rows, rows),
        check_vma=False,
    )
```
